32 devices in a mesh: fsdp: 32 (over z, y, x, core).
Axes of the slice: x: 2, y: 2, z: 4, core: 2. Of those that a mesh axis runs over, the one named last changes fastest.
Arguments:
- tokens: bfloat16 [4096, 960], P('fsdp'), may hold values from -6 to 6
- cotangent: bfloat16 [4096, 960], P('fsdp'), may hold values from -6 to 6
- seq_lengths: int32 [64], replicated, may hold values from 16 to 112, as said below
- seq_owner: int32 [64], replicated, may hold values from 0 to 31, as said below
- query_weight: bfloat16 [921600], P('fsdp'), may hold values from -0.1875 to 0.1875
- key_weight: bfloat16 [307200], P('fsdp'), may hold values from -0.1875 to 0.1875
- value_weight: bfloat16 [307200], P('fsdp'), may hold values from -0.1875 to 0.1875
- out_weight: bfloat16 [921600], P('fsdp'), may hold values from -0.5 to 0.5
- gate_weight: bfloat16 [2457600], P('fsdp'), may hold values from -0.1875 to 0.1875
- up_weight: bfloat16 [2457600], P('fsdp'), may hold values from -0.1875 to 0.1875
- down_weight: bfloat16 [2457600], P('fsdp'), may hold values from -0.125 to 0.125
- attention_gain: float32 [960], replicated, may hold values from 0.5 to 1.5
- feedforward_gain: float32 [960], replicated, may hold values from 0.5 to 1.5
Outputs:
- layer_out: bfloat16 [4096, 960], P('fsdp')
- grad_tokens: bfloat16 [4096, 960], P('fsdp')
- grad_query_weight: float32 [921600], P('fsdp')
- grad_key_weight: float32 [307200], P('fsdp')
- grad_value_weight: float32 [307200], P('fsdp')
- grad_out_weight: float32 [921600], P('fsdp')
- grad_gate_weight: float32 [2457600], P('fsdp')
- grad_up_weight: float32 [2457600], P('fsdp')
- grad_down_weight: float32 [2457600], P('fsdp')
- grad_attention_gain: float32 [960], replicated
- grad_feedforward_gain: float32 [960], replicated
The draws below stay inside these ranges and needn't reach their ends.
Inputs may be any that keep to these rules, and one draw needn't show every extreme that they name: `seq_lengths`: every device holds exactly two sequences, and the two lengths of a device sum to at most 128; some device is full in every draw. `seq_owner`: each device number appears exactly twice.
All inputs are finite; a program needn't handle non-finite values.
Results may differ from the reference program's by a relative error of at most 0.015.
Values may be sent and summed in bfloat16 or wider, within the bound.
A program may use at most 256 MiB of HBM per device.

```python
import math
from functools import partial
import jax
import jax.numpy as jnp
from jax import lax

D = 960
HEADS = 15
KV_HEADS = 5
HD = 64
FF = 2560
TOK_DEV = 128
LEAST = 16
TOKENS = 4096
N_FSDP = 32


def deal_helper(key):
    device_count = N_FSDP
    shuffled = jax.random.permutation(jax.random.fold_in(key, 11), 2 * device_count)
    totals = jax.random.randint(jax.random.fold_in(key, 12), (device_count,), TOK_DEV // 2, TOK_DEV + 1)
    spread = jax.random.randint(jax.random.fold_in(key, 13), (device_count,), 0, 1 << 20)
    fullest = jax.random.randint(jax.random.fold_in(key, 14), (), 0, device_count)
    device_ids = jnp.arange(device_count)
    totals = jnp.where(device_ids == fullest, TOK_DEV, totals)
    firsts = LEAST + spread % (totals - 2 * LEAST + 1)
    firsts = jnp.where(device_ids == fullest, TOK_DEV - LEAST, firsts)
    owners = shuffled // 2
    slot_side = shuffled % 2
    own_total = totals[owners]
    own_first = firsts[owners]
    lengths = jnp.where(slot_side == 0, own_first, own_total - own_first)
    return (lengths.astype(jnp.int32), owners.astype(jnp.int32))


def draw_seq_lengths(key, part):
    return deal_helper(key)[0]


def draw_seq_owner(key, part):
    return deal_helper(key)[1]


def block_levels(rng, extent, cuts, least, high):
    gain, own = 1.0, jax.random.fold_in(rng, 6)
    for dim, blocks in cuts:
        steps = jnp.exp(jax.random.uniform(jax.random.fold_in(own, dim), (blocks,), jnp.float32, least / len(cuts), high / len(cuts)))
        gain = gain * jnp.repeat(steps, extent[dim] // blocks).reshape([-1 if axis == dim else 1 for axis in range(len(extent))])
    return gain


def normal_values(stream_key, dims, deviation, limit, split=(), kind=jnp.bfloat16):
    drawn = deviation * jax.random.normal(stream_key, dims, jnp.float32)
    if split:
        drawn = drawn * block_levels(stream_key, dims, split, -0.22, 0.18)
    return jnp.clip(drawn, -limit, limit).astype(kind)


def setup_inputs(seed: int = 0) -> dict:
    key_list = jax.random.split(jax.random.key(seed), 14)
    tokens = normal_values(key_list[0], (TOKENS, D), 1.0, 6.0, ((0, 32),))
    cotangent = normal_values(key_list[1], (TOKENS, D), 1.0, 6.0, ((0, 32),))
    seq_lengths = draw_seq_lengths(jax.random.fold_in(key_list[13], 71), 0)
    seq_owner = draw_seq_owner(jax.random.fold_in(key_list[13], 71), 0)
    query_weight = normal_values(key_list[4], (D * HEADS * HD,), D ** -0.5, 0.1875, ((0, 32),))
    key_weight = normal_values(key_list[5], (D * KV_HEADS * HD,), D ** -0.5, 0.1875, ((0, 32),))
    value_weight = normal_values(key_list[6], (D * KV_HEADS * HD,), D ** -0.5, 0.1875, ((0, 32),))
    out_weight = normal_values(key_list[7], (HEADS * HD * D,), (HEADS * HD // 8) ** -0.5, 0.5, ((0, 32),))
    gate_weight = normal_values(key_list[8], (D * FF,), D ** -0.5, 0.1875, ((0, 32),))
    up_weight = normal_values(key_list[9], (D * FF,), D ** -0.5, 0.1875, ((0, 32),))
    down_weight = normal_values(key_list[10], (FF * D,), FF ** -0.5, 0.125, ((0, 32),))
    attention_gain = jnp.clip(1.0 + 0.1 * jax.random.normal(key_list[11], (D,), jnp.float32), 0.5, 1.5)
    feedforward_gain = jnp.clip(1.0 + 0.1 * jax.random.normal(key_list[12], (D,), jnp.float32), 0.5, 1.5)
    return {"tokens": tokens, "cotangent": cotangent, "seq_lengths": seq_lengths, "seq_owner": seq_owner, "query_weight": query_weight, "key_weight": key_weight, "value_weight": value_weight, "out_weight": out_weight, "gate_weight": gate_weight, "up_weight": up_weight, "down_weight": down_weight, "attention_gain": attention_gain, "feedforward_gain": feedforward_gain}


EPSILON = 1e-05
ROPE_BASE = 10000.0
MASKED_SCORE = -1e+30

@jax.custom_vjp
def low(v):
    return lax.optimization_barrier(v.astype(jnp.bfloat16)).astype(jnp.float32)

@jax.custom_vjp
def low_back(v):
    return v

def low_keep(v):
    return (low(v), None)

def low_pass(kept, grad):
    return (grad,)

def back_keep(v):
    return (v, None)

def back_low(kept, grad):
    return (low(grad),)
low.defvjp(low_keep, low_pass)
low_back.defvjp(back_keep, back_low)

def own_rows(seq_lengths, seq_owner, device, row_count):
    seq_count = seq_lengths.shape[0]
    seq_index = jnp.arange(seq_count, dtype=jnp.int32)
    is_mine = seq_owner == device
    first_seq = jnp.min(jnp.where(is_mine, seq_index, seq_count))
    second_seq = jnp.min(jnp.where(is_mine & (seq_index != first_seq), seq_index, seq_count))
    len_first = jnp.sum(jnp.where(seq_index == first_seq, seq_lengths, 0))
    len_second = jnp.sum(jnp.where(seq_index == second_seq, seq_lengths, 0))
    row_index = jnp.arange(row_count, dtype=jnp.int32)
    segment = (row_index >= len_first).astype(jnp.int32) + (row_index >= len_first + len_second).astype(jnp.int32)
    seg_start = jnp.where(segment == 0, 0, jnp.where(segment == 1, len_first, len_first + len_second))
    position = row_index - seg_start
    row_valid = (segment < 2).astype(jnp.float32)
    allowed = (segment[:, None] == segment[None, :]) & (row_index[None, :] <= row_index[:, None])
    return (position, row_valid, allowed)

def rope_tables(position, head_size):
    half_size = head_size // 2
    frequency = ROPE_BASE ** (-jnp.arange(half_size, dtype=jnp.float32) * 2.0 / head_size)
    angles = position.astype(jnp.float32)[:, None] * frequency[None, :]
    return (jnp.cos(angles), jnp.sin(angles))

def rotate(values, cosine, sine_table):
    half_size = values.shape[-1] // 2
    front_half = values[..., :half_size]
    back_half = values[..., half_size:]
    cos_part = cosine[:, None, :]
    sin_part = sine_table[:, None, :]
    return jnp.concatenate([front_half * cos_part - back_half * sin_part, back_half * cos_part + front_half * sin_part], axis=-1)

def rms_scale(values):
    return lax.rsqrt(lax.optimization_barrier(jnp.mean(values * values, axis=-1, keepdims=True)) + EPSILON)

def exact_dot(left_side, right_side):
    return jnp.dot(left_side, right_side, precision=lax.Precision.HIGHEST)

def block_forward(weights, gain_pair, seq_lengths, seq_owner, block_pair):
    row_block, device = block_pair
    w_query, w_key, w_value, w_out, w_gate, w_up, w_down = weights
    gain_one, gain_two = gain_pair
    groups = HEADS // KV_HEADS
    position, row_valid, allowed = own_rows(seq_lengths, seq_owner, device, TOK_DEV)
    cosine, sine_table = rope_tables(position, HD)
    scale_one = rms_scale(row_block)
    normed_one = row_block * scale_one
    low_one = low(normed_one * gain_one)
    query_pre = low_back(exact_dot(low_one, w_query.reshape(D, HEADS * HD))).reshape(TOK_DEV, HEADS, HD)
    key_pre = low_back(exact_dot(low_one, w_key.reshape(D, KV_HEADS * HD))).reshape(TOK_DEV, KV_HEADS, HD)
    value_low = low_back(low(exact_dot(low_one, w_value.reshape(D, KV_HEADS * HD)))).reshape(TOK_DEV, KV_HEADS, HD)
    query_low = low(rotate(query_pre, cosine, sine_table)).reshape(TOK_DEV, KV_HEADS, groups, HD)
    key_low = low(rotate(key_pre, cosine, sine_table))
    score_scale = 1.0 / math.sqrt(HD)
    scores = low_back(jnp.einsum('ikgd,jkd->kgij', query_low, key_low, precision=lax.Precision.HIGHEST) * score_scale)
    masked = jnp.where(allowed[None, None], scores, MASKED_SCORE)
    row_max = lax.optimization_barrier(jnp.max(masked, axis=-1, keepdims=True))
    exp_scores = jnp.exp(masked - row_max)
    prob_rows = exp_scores / lax.optimization_barrier(jnp.sum(exp_scores, axis=-1, keepdims=True))
    attended = jnp.einsum('kgij,jkd->ikgd', low(prob_rows), value_low, precision=lax.Precision.HIGHEST)
    attended_low = low_back(low(attended.reshape(TOK_DEV, HEADS * HD)))
    middle = row_block + low_back(exact_dot(attended_low, w_out.reshape(HEADS * HD, D)))
    scale_two = rms_scale(middle)
    normed_two = middle * scale_two
    low_two = low(normed_two * gain_two)
    gate_pre = low_back(exact_dot(low_two, w_gate.reshape(D, FF)))
    upward = low_back(exact_dot(low_two, w_up.reshape(D, FF)))
    hidden_low = low_back(low(jax.nn.silu(gate_pre) * upward))
    branch_two = low_back(exact_dot(hidden_low, w_down.reshape(FF, D)))
    return row_valid[:, None] * (middle + branch_two)

def layer_forward(inputs, w_query, w_key, w_value, w_out, w_gate, w_up, w_down, gain_one, gain_two, seq_lengths, seq_owner):
    weights = (w_query, w_key, w_value, w_out, w_gate, w_up, w_down)
    blocks = inputs.reshape(N_FSDP, TOK_DEV, D)
    device_ids = jnp.arange(N_FSDP, dtype=jnp.int32)
    stepper = jax.checkpoint(partial(block_forward, weights, (gain_one, gain_two), seq_lengths, seq_owner))
    result = lax.map(stepper, (blocks, device_ids))
    return result.reshape(TOKENS, D)

def reference(tokens, cotangent, seq_lengths, seq_owner, query_weight, key_weight, value_weight, out_weight, gate_weight, up_weight, down_weight, attention_gain, feedforward_gain):
    floats = (tokens.astype(jnp.float32), query_weight.astype(jnp.float32), key_weight.astype(jnp.float32), value_weight.astype(jnp.float32), out_weight.astype(jnp.float32), gate_weight.astype(jnp.float32), up_weight.astype(jnp.float32), down_weight.astype(jnp.float32), attention_gain.astype(jnp.float32), feedforward_gain.astype(jnp.float32))
    primal = partial(layer_forward, seq_lengths=seq_lengths, seq_owner=seq_owner)
    outputs, pullback = jax.vjp(primal, *floats)
    gradient = pullback(cotangent.astype(jnp.float32))
    return (outputs.astype(jnp.bfloat16), gradient[0].astype(jnp.bfloat16), gradient[1], gradient[2], gradient[3], gradient[4], gradient[5], gradient[6], gradient[7], gradient[8], gradient[9])
```

```python
import math

import jax
import jax.numpy as jnp
from jax import lax
from jax.sharding import PartitionSpec as P

D = 960
HEADS = 15
KV_HEADS = 5
HD = 64
FF = 2560


EPSILON = 1e-05
ROPE_BASE = 10000.0
MASKED_SCORE = -1e30


def own_rows(seq_lengths, seq_owner, device, row_count):
    seq_count = seq_lengths.shape[0]
    seq_index = jnp.arange(seq_count, dtype=jnp.int32)
    is_mine = seq_owner == device
    first_seq = jnp.min(jnp.where(is_mine, seq_index, seq_count))
    second_seq = jnp.min(jnp.where(is_mine & (seq_index != first_seq), seq_index, seq_count))
    len_first = jnp.sum(jnp.where(seq_index == first_seq, seq_lengths, 0))
    len_second = jnp.sum(jnp.where(seq_index == second_seq, seq_lengths, 0))
    row_index = jnp.arange(row_count, dtype=jnp.int32)
    segment = (row_index >= len_first).astype(jnp.int32) + (
        row_index >= len_first + len_second
    ).astype(jnp.int32)
    seg_start = jnp.where(
        segment == 0, 0, jnp.where(segment == 1, len_first, len_first + len_second)
    )
    position = row_index - seg_start
    row_valid = (segment < 2).astype(jnp.float32)
    allowed = (segment[:, None] == segment[None, :]) & (row_index[None, :] <= row_index[:, None])
    return (position, row_valid, allowed)


def rope_tables(position, head_size):
    half_size = head_size // 2
    frequency = ROPE_BASE ** (-jnp.arange(half_size, dtype=jnp.float32) * 2.0 / head_size)
    angles = position.astype(jnp.float32)[:, None] * frequency[None, :]
    return (jnp.cos(angles), jnp.sin(angles))


def rotate(values, cosine, sine_table):
    half_size = values.shape[-1] // 2
    front_half = values[..., :half_size]
    back_half = values[..., half_size:]
    cos_part = cosine[:, None, :]
    sin_part = sine_table[:, None, :]
    return jnp.concatenate(
        [
            front_half * cos_part - back_half * sin_part,
            back_half * cos_part + front_half * sin_part,
        ],
        axis=-1,
    )


def unrotate(gradient, cosine, sine_table):
    half_size = gradient.shape[-1] // 2
    front_half = gradient[..., :half_size]
    back_half = gradient[..., half_size:]
    cos_part = cosine[:, None, :]
    sin_part = sine_table[:, None, :]
    return jnp.concatenate(
        [
            front_half * cos_part + back_half * sin_part,
            back_half * cos_part - front_half * sin_part,
        ],
        axis=-1,
    )


def rms_scale(values):
    return lax.rsqrt(jnp.mean(values * values, axis=-1, keepdims=True) + EPSILON)


def outer_sum(left_side, right_side):
    return lax.dot_general(
        left_side, right_side, (((0,), (0,)), ((), ())), preferred_element_type=jnp.float32
    )


def times_t(left_side, right_side):
    return lax.dot_general(
        left_side, right_side, (((1,), (1,)), ((), ())), preferred_element_type=jnp.float32
    )


def pack_shards(shard_list):
    return jnp.concatenate([piece.reshape(1, -1) for piece in shard_list], axis=1)


def unpack_gathered(whole, shard_list):
    result_list = []
    offset = 0
    for piece in shard_list:
        width = piece.shape[0]
        result_list.append(whole[:, offset : offset + width].reshape(-1))
        offset = offset + width
    return result_list


def pack_grads(grad_list, count):
    return jnp.concatenate([item.reshape(count, -1) for item in grad_list], axis=1)


def unpack_grads(summed, grad_list, count):
    result_list = []
    offset = 0
    for item in grad_list:
        width = item.size // count
        result_list.append(summed[:, offset : offset + width].reshape(-1))
        offset = offset + width
    return result_list


def shape_weights(flat_list):
    query_flat, key_flat, value_flat, out_flat, gate_flat, up_flat, down_flat = flat_list
    return (
        query_flat.reshape(D, HEADS * HD),
        key_flat.reshape(D, KV_HEADS * HD),
        value_flat.reshape(D, KV_HEADS * HD),
        out_flat.reshape(HEADS * HD, D),
        gate_flat.reshape(D, FF),
        up_flat.reshape(D, FF),
        down_flat.reshape(FF, D),
    )


def on_device(
    tokens,
    cotangent,
    seq_lengths,
    seq_owner,
    query_weight,
    key_weight,
    value_weight,
    out_weight,
    gate_weight,
    up_weight,
    down_weight,
    attention_gain,
    feedforward_gain,
):
    row_count = tokens.shape[0]
    groups = HEADS // KV_HEADS
    score_scale = 1.0 / math.sqrt(HD)
    count = lax.axis_size("fsdp")
    device = lax.axis_index("fsdp")
    position, row_valid, allowed = own_rows(seq_lengths, seq_owner, device, row_count)
    cosine, sine_table = rope_tables(position, HD)
    shard_list = (
        query_weight,
        key_weight,
        value_weight,
        out_weight,
        gate_weight,
        up_weight,
        down_weight,
    )
    gathered = lax.all_gather(pack_shards(shard_list), "fsdp", axis=0, tiled=True)
    w_query, w_key, w_value, w_out, w_gate, w_up, w_down = shape_weights(
        unpack_gathered(gathered, shard_list)
    )
    inputs = tokens.astype(jnp.float32)
    scale_one = rms_scale(inputs)
    normed_one = inputs * scale_one
    low_one = (normed_one * attention_gain).astype(jnp.bfloat16)
    query_pre = jnp.dot(low_one, w_query, preferred_element_type=jnp.float32).reshape(
        row_count, HEADS, HD
    )
    key_pre = jnp.dot(low_one, w_key, preferred_element_type=jnp.float32).reshape(
        row_count, KV_HEADS, HD
    )
    value_low = (
        jnp.dot(low_one, w_value, preferred_element_type=jnp.float32)
        .astype(jnp.bfloat16)
        .reshape(row_count, KV_HEADS, HD)
    )
    query_low = (
        rotate(query_pre, cosine, sine_table)
        .astype(jnp.bfloat16)
        .reshape(row_count, KV_HEADS, groups, HD)
    )
    key_low = rotate(key_pre, cosine, sine_table).astype(jnp.bfloat16)
    scores = (
        jnp.einsum("ikgd,jkd->kgij", query_low, key_low, preferred_element_type=jnp.float32)
        * score_scale
    )
    masked = jnp.where(allowed[None, None], scores, MASKED_SCORE)
    row_max = jnp.max(masked, axis=-1, keepdims=True)
    exp_scores = jnp.exp(masked - row_max)
    row_total = jnp.sum(exp_scores, axis=-1, keepdims=True)
    log_total = row_max + jnp.log(row_total)
    prob_rows = (exp_scores / row_total).astype(jnp.bfloat16)
    attended = jnp.einsum(
        "kgij,jkd->ikgd", prob_rows, value_low, preferred_element_type=jnp.float32
    )
    attended_low = attended.reshape(row_count, HEADS * HD).astype(jnp.bfloat16)
    middle = inputs + jnp.dot(attended_low, w_out, preferred_element_type=jnp.float32)
    scale_two = rms_scale(middle)
    normed_two = middle * scale_two
    low_two = (normed_two * feedforward_gain).astype(jnp.bfloat16)
    gate_pre = jnp.dot(low_two, w_gate, preferred_element_type=jnp.float32)
    upward = jnp.dot(low_two, w_up, preferred_element_type=jnp.float32)
    sigmoid_gate = jax.nn.sigmoid(gate_pre)
    silu_gate = gate_pre * sigmoid_gate
    hidden_low = (silu_gate * upward).astype(jnp.bfloat16)
    branch_two = jnp.dot(hidden_low, w_down, preferred_element_type=jnp.float32)
    layer_out = (row_valid[:, None] * (middle + branch_two)).astype(jnp.bfloat16)
    grad_out = row_valid[:, None] * cotangent.astype(jnp.float32)
    grad_out_low = grad_out.astype(jnp.bfloat16)
    grad_wdown = outer_sum(hidden_low, grad_out_low)
    grad_hidden = times_t(grad_out_low, w_down).astype(jnp.bfloat16).astype(jnp.float32)
    grad_up = (grad_hidden * silu_gate).astype(jnp.bfloat16)
    grad_gate = (
        grad_hidden * upward * sigmoid_gate * (1.0 + gate_pre * (1.0 - sigmoid_gate))
    ).astype(jnp.bfloat16)
    grad_wgate = outer_sum(low_two, grad_gate)
    grad_wup = outer_sum(low_two, grad_up)
    grad_norm_two = times_t(grad_gate, w_gate) + times_t(grad_up, w_up)
    grad_gain_two = jnp.sum(grad_norm_two * normed_two, axis=0)
    scaled_two = grad_norm_two * feedforward_gain
    grad_middle = grad_out + scale_two * (
        scaled_two - normed_two * jnp.mean(scaled_two * normed_two, axis=-1, keepdims=True)
    )
    grad_branch_low = grad_middle.astype(jnp.bfloat16)
    grad_wout = outer_sum(attended_low, grad_branch_low)
    grad_attended = (
        times_t(grad_branch_low, w_out)
        .astype(jnp.bfloat16)
        .reshape(row_count, KV_HEADS, groups, HD)
    )
    scores_again = (
        jnp.einsum("ikgd,jkd->kgij", query_low, key_low, preferred_element_type=jnp.float32)
        * score_scale
    )
    probs_again = jnp.exp(jnp.where(allowed[None, None], scores_again, MASKED_SCORE) - log_total)
    grad_value = jnp.einsum(
        "kgij,ikgd->jkd",
        probs_again.astype(jnp.bfloat16),
        grad_attended,
        preferred_element_type=jnp.float32,
    )
    grad_probs = jnp.einsum(
        "ikgd,jkd->kgij", grad_attended, value_low, preferred_element_type=jnp.float32
    )
    inner_sum = jnp.sum(probs_again * grad_probs, axis=-1, keepdims=True)
    grad_scores = (probs_again * (grad_probs - inner_sum)).astype(jnp.bfloat16)
    grad_query = (
        jnp.einsum("kgij,jkd->ikgd", grad_scores, key_low, preferred_element_type=jnp.float32)
        * score_scale
    )
    grad_key = (
        jnp.einsum("kgij,ikgd->jkd", grad_scores, query_low, preferred_element_type=jnp.float32)
        * score_scale
    )
    grad_query_low = (
        unrotate(grad_query.reshape(row_count, HEADS, HD), cosine, sine_table)
        .reshape(row_count, HEADS * HD)
        .astype(jnp.bfloat16)
    )
    grad_key_low = (
        unrotate(grad_key, cosine, sine_table)
        .reshape(row_count, KV_HEADS * HD)
        .astype(jnp.bfloat16)
    )
    grad_value_low = grad_value.reshape(row_count, KV_HEADS * HD).astype(jnp.bfloat16)
    grad_wquery = outer_sum(low_one, grad_query_low)
    grad_wkey = outer_sum(low_one, grad_key_low)
    grad_wvalue = outer_sum(low_one, grad_value_low)
    grad_norm_one = (
        times_t(grad_query_low, w_query)
        + times_t(grad_key_low, w_key)
        + times_t(grad_value_low, w_value)
    )
    grad_gain_one = jnp.sum(grad_norm_one * normed_one, axis=0)
    scaled_one = grad_norm_one * attention_gain
    grad_inputs = grad_middle + scale_one * (
        scaled_one - normed_one * jnp.mean(scaled_one * normed_one, axis=-1, keepdims=True)
    )
    gain_one_sum, gain_two_sum = lax.psum((grad_gain_one, grad_gain_two), "fsdp")
    every_list = (grad_wquery, grad_wkey, grad_wvalue, grad_wout, grad_wgate, grad_wup, grad_wdown)
    every_summed = lax.psum_scatter(
        pack_grads(every_list, count), "fsdp", scatter_dimension=0, tiled=True
    )
    query_shard, key_shard, value_shard, out_shard, gate_shard, up_shard, down_shard = unpack_grads(
        every_summed, every_list, count
    )
    return (
        layer_out,
        grad_inputs.astype(jnp.bfloat16),
        query_shard,
        key_shard,
        value_shard,
        out_shard,
        gate_shard,
        up_shard,
        down_shard,
        gain_one_sum,
        gain_two_sum,
    )


BLOCK = 32


def pad_rows(block, spare):
    return jnp.pad(block, ((0, spare), (0, 0)))


def spread(values, count):
    rows = values.shape[0]
    wide = values.reshape(rows, count, -1)
    return jnp.pad(wide, ((0, 0), (0, 0), (0, BLOCK - wide.shape[2]))).reshape(rows, count * BLOCK)


def gather_in(values, count, width):
    rows = values.shape[0]
    return values.reshape(rows, count, BLOCK)[:, :, :width].reshape(rows, count * width)


def paired_on_device(
    tokens,
    cotangent,
    seq_lengths,
    seq_owner,
    query_weight,
    key_weight,
    value_weight,
    out_weight,
    gate_weight,
    up_weight,
    down_weight,
    attention_gain,
    feedforward_gain,
):
    row_count = tokens.shape[0]
    groups = HEADS // KV_HEADS
    score_scale = 1.0 / math.sqrt(HD)
    count = lax.axis_size("fsdp")
    chips = count // 2
    width = D // count
    units = FF // count
    spare = BLOCK - width
    device = lax.axis_index("fsdp")
    core = device % 2
    swap = [(i, i ^ 1) for i in range(count)]
    chip_groups = [[2 * k + side for k in range(chips)] for side in range(2)]

    def other_core(values):
        return lax.ppermute(values, "fsdp", swap)

    def in_core_order(mine, theirs, axis):
        return jnp.where(
            core == 0,
            jnp.concatenate([mine, theirs], axis=axis),
            jnp.concatenate([theirs, mine], axis=axis),
        )

    def take_core(pair, index):
        return lax.dynamic_index_in_dim(pair, index, axis=0, keepdims=False)

    def gather_chips(block):
        return lax.all_gather(block, "fsdp", axis_index_groups=chip_groups, axis=0, tiled=False)

    def scatter_chips(blocks):
        return lax.psum_scatter(
            blocks,
            "fsdp",
            scatter_dimension=0,
            axis_index_groups=chip_groups,
            tiled=False,
        )

    attention_shard = pad_rows(
        jnp.concatenate(
            [
                query_weight.reshape(width, HEADS * HD),
                key_weight.reshape(width, KV_HEADS * HD),
                value_weight.reshape(width, KV_HEADS * HD),
                out_weight.reshape(width, D),
            ],
            axis=1,
        ),
        spare,
    )
    attention_mine = gather_chips(attention_shard)
    attention_other = other_core(attention_mine)

    gate_up = jnp.stack([gate_weight.reshape(width, chips, 2, units), up_weight.reshape(width, chips, 2, units)])
    gate_up = gate_up.transpose(3, 0, 1, 2, 4).reshape(2, 2, width, chips * units)
    gate_up = jnp.pad(gate_up, ((0, 0), (0, 0), (0, spare), (0, 0)))
    gate_up_other = other_core(take_core(gate_up, 1 - core))
    gate_up_pair = in_core_order(take_core(gate_up, core), gate_up_other, 1)
    gate_up_all = gather_chips(gate_up_pair)
    w_gate = gate_up_all[:, 0].reshape(count * BLOCK, chips * units)
    w_up = gate_up_all[:, 1].reshape(count * BLOCK, chips * units)
    w_down = gather_chips(down_weight.reshape(units, D)).reshape(chips * units, D)

    attention_all = in_core_order(attention_mine[:, None], attention_other[:, None], 1).reshape(
        count * BLOCK, 2 * HEADS * HD + 2 * KV_HEADS * HD
    )
    wide_qkv = (HEADS + 2 * KV_HEADS) * HD
    w_qkv = attention_all[:, :wide_qkv]
    w_out = attention_all[:, wide_qkv:]

    position, row_valid, allowed = own_rows(seq_lengths, seq_owner, device, row_count)
    cosine, sine_table = rope_tables(position, HD)
    grad_out = row_valid[:, None] * cotangent.astype(jnp.float32)
    grad_out_low = grad_out.astype(jnp.bfloat16)
    grad_out_both = jnp.concatenate([grad_out_low, other_core(grad_out_low)], axis=0)

    inputs = tokens.astype(jnp.float32)
    scale_one = rms_scale(inputs)
    normed_one = inputs * scale_one
    low_one = spread((normed_one * attention_gain).astype(jnp.bfloat16), count)
    qkv = jnp.dot(low_one, w_qkv, preferred_element_type=jnp.float32)
    query_pre = qkv[:, : HEADS * HD].reshape(row_count, HEADS, HD)
    key_pre = qkv[:, HEADS * HD : (HEADS + KV_HEADS) * HD].reshape(row_count, KV_HEADS, HD)
    value_low = qkv[:, (HEADS + KV_HEADS) * HD :].astype(jnp.bfloat16).reshape(row_count, KV_HEADS, HD)
    query_low = (
        rotate(query_pre, cosine, sine_table)
        .astype(jnp.bfloat16)
        .reshape(row_count, KV_HEADS, groups, HD)
    )
    key_low = rotate(key_pre, cosine, sine_table).astype(jnp.bfloat16)
    scores = (
        jnp.einsum("ikgd,jkd->kgij", query_low, key_low, preferred_element_type=jnp.float32)
        * score_scale
    )
    masked = jnp.where(allowed[None, None], scores, MASKED_SCORE)
    row_max = jnp.max(masked, axis=-1, keepdims=True)
    exp_scores = jnp.exp(masked - row_max)
    row_total = jnp.sum(exp_scores, axis=-1, keepdims=True)
    probs = exp_scores / row_total
    prob_rows = probs.astype(jnp.bfloat16)
    attended = jnp.einsum(
        "kgij,jkd->ikgd", prob_rows, value_low, preferred_element_type=jnp.float32
    )
    attended_low = spread(attended.reshape(row_count, HEADS * HD).astype(jnp.bfloat16), count)
    middle = inputs + jnp.dot(attended_low, w_out, preferred_element_type=jnp.float32)
    scale_two = rms_scale(middle)
    normed_two = middle * scale_two
    low_two = spread((normed_two * feedforward_gain).astype(jnp.bfloat16), count)
    low_two_both = jnp.concatenate([low_two, other_core(low_two)], axis=0)

    gate_pre = jnp.dot(low_two_both, w_gate, preferred_element_type=jnp.float32)
    upward = jnp.dot(low_two_both, w_up, preferred_element_type=jnp.float32)
    sigmoid_gate = jax.nn.sigmoid(gate_pre)
    silu_gate = gate_pre * sigmoid_gate
    hidden_low = (silu_gate * upward).astype(jnp.bfloat16)
    branch_both = jnp.dot(hidden_low, w_down, preferred_element_type=jnp.float32)
    branch_two = branch_both[:row_count] + other_core(branch_both[row_count:])
    layer_out = (row_valid[:, None] * (middle + branch_two)).astype(jnp.bfloat16)

    grad_wdown = outer_sum(hidden_low, grad_out_both).astype(jnp.bfloat16)
    down_sum = scatter_chips(grad_wdown.reshape(chips, units, D))
    grad_hidden = times_t(grad_out_both, w_down).astype(jnp.bfloat16).astype(jnp.float32)
    grad_up = (grad_hidden * silu_gate).astype(jnp.bfloat16)
    grad_gate = (
        grad_hidden * upward * sigmoid_gate * (1.0 + gate_pre * (1.0 - sigmoid_gate))
    ).astype(jnp.bfloat16)
    grad_wgate = outer_sum(low_two_both, grad_gate).astype(jnp.bfloat16)
    grad_wup = outer_sum(low_two_both, grad_up).astype(jnp.bfloat16)
    gate_up_sum = scatter_chips(
        jnp.concatenate(
            [
                grad_wgate.reshape(chips, 2 * BLOCK, chips * units),
                grad_wup.reshape(chips, 2 * BLOCK, chips * units),
            ],
            axis=1,
        )
    )
    grad_norm_both = times_t(grad_gate, w_gate) + times_t(grad_up, w_up)
    grad_norm_two = gather_in(
        grad_norm_both[:row_count] + other_core(grad_norm_both[row_count:]), count, width
    )
    grad_gain_two = jnp.sum(grad_norm_two * normed_two, axis=0)
    scaled_two = grad_norm_two * feedforward_gain
    grad_middle = grad_out + scale_two * (
        scaled_two - normed_two * jnp.mean(scaled_two * normed_two, axis=-1, keepdims=True)
    )
    grad_branch_low = grad_middle.astype(jnp.bfloat16)
    grad_wout = outer_sum(attended_low, grad_branch_low)
    grad_attended = gather_in(
        times_t(grad_branch_low, w_out).astype(jnp.bfloat16), count, width
    ).reshape(row_count, KV_HEADS, groups, HD)
    grad_value = jnp.einsum(
        "kgij,ikgd->jkd", prob_rows, grad_attended, preferred_element_type=jnp.float32
    )
    grad_probs = jnp.einsum(
        "ikgd,jkd->kgij", grad_attended, value_low, preferred_element_type=jnp.float32
    )
    inner_sum = jnp.sum(probs * grad_probs, axis=-1, keepdims=True)
    grad_scores = (probs * (grad_probs - inner_sum)).astype(jnp.bfloat16)
    grad_query = (
        jnp.einsum("kgij,jkd->ikgd", grad_scores, key_low, preferred_element_type=jnp.float32)
        * score_scale
    )
    grad_key = (
        jnp.einsum("kgij,ikgd->jkd", grad_scores, query_low, preferred_element_type=jnp.float32)
        * score_scale
    )
    grad_qkv = jnp.concatenate(
        [
            unrotate(grad_query.reshape(row_count, HEADS, HD), cosine, sine_table)
            .reshape(row_count, HEADS * HD)
            .astype(jnp.bfloat16),
            unrotate(grad_key, cosine, sine_table)
            .reshape(row_count, KV_HEADS * HD)
            .astype(jnp.bfloat16),
            grad_value.reshape(row_count, KV_HEADS * HD).astype(jnp.bfloat16),
        ],
        axis=1,
    )
    grad_wqkv = outer_sum(low_one, grad_qkv)
    grad_attention = jnp.concatenate([grad_wqkv, grad_wout], axis=1).reshape(
        chips, 2, BLOCK, 2 * HEADS * HD + 2 * KV_HEADS * HD
    )
    keep = lax.dynamic_index_in_dim(grad_attention, core, axis=1, keepdims=False)
    give = lax.dynamic_index_in_dim(grad_attention, 1 - core, axis=1, keepdims=False)
    attention_sum = scatter_chips(
        (keep + other_core(give.astype(jnp.bfloat16)).astype(jnp.float32)).astype(jnp.bfloat16)
    )[:width].astype(jnp.float32)

    grad_norm_one = gather_in(times_t(grad_qkv, w_qkv), count, width)
    grad_gain_one = jnp.sum(grad_norm_one * normed_one, axis=0)
    scaled_one = grad_norm_one * attention_gain
    grad_inputs = grad_middle + scale_one * (
        scaled_one - normed_one * jnp.mean(scaled_one * normed_one, axis=-1, keepdims=True)
    )
    gain_sums = jnp.sum(
        lax.all_gather(jnp.stack([grad_gain_one, grad_gain_two]), "fsdp", axis=0), axis=0
    )

    gate_up_sum = gate_up_sum.reshape(2, 2, BLOCK, chips * units).transpose(1, 0, 2, 3)
    gate_up_got = other_core(take_core(gate_up_sum, 1 - core))
    gate_up_kept = take_core(gate_up_sum, core)
    halves = in_core_order(gate_up_kept[None], gate_up_got[None], 0)[:, :, :width]
    halves = halves.reshape(2, 2, width, chips, units).transpose(1, 2, 3, 0, 4).astype(jnp.float32)
    edge_key, edge_value = HEADS * HD, (HEADS + KV_HEADS) * HD
    return (
        layer_out,
        grad_inputs.astype(jnp.bfloat16),
        attention_sum[:, :edge_key].reshape(-1),
        attention_sum[:, edge_key:edge_value].reshape(-1),
        attention_sum[:, edge_value:wide_qkv].reshape(-1),
        attention_sum[:, wide_qkv:].reshape(-1),
        halves[0].reshape(-1),
        halves[1].reshape(-1),
        down_sum.astype(jnp.float32).reshape(-1),
        gain_sums[0],
        gain_sums[1],
    )


def solution(mesh):
    count = mesh.shape["fsdp"]
    whole_rows = count % 2 == 0 and D % count == 0 and FF % count == 0 and D // count <= BLOCK
    program = paired_on_device if whole_rows else on_device
    return jax.shard_map(
        program,
        mesh=mesh,
        in_specs=(
            P("fsdp", None),
            P("fsdp", None),
            P(),
            P(),
            P("fsdp"),
            P("fsdp"),
            P("fsdp"),
            P("fsdp"),
            P("fsdp"),
            P("fsdp"),
            P("fsdp"),
            P(),
            P(),
        ),
        out_specs=(
            P("fsdp", None),
            P("fsdp", None),
            P("fsdp"),
            P("fsdp"),
            P("fsdp"),
            P("fsdp"),
            P("fsdp"),
            P("fsdp"),
            P("fsdp"),
            P(),
            P(),
        ),
        check_vma=False,
    )
```

```python
import math

import jax
import jax.numpy as jnp
from jax import lax
from jax.experimental import pallas as pl
from jax.experimental.pallas import tpu as pltpu
from jax.sharding import PartitionSpec as P

D = 960
HEADS = 15
KV_HEADS = 5
HD = 64
FF = 2560


EPSILON = 1e-05
ROPE_BASE = 10000.0
MASKED_SCORE = -1e30


def own_rows(seq_lengths, seq_owner, device, row_count):
    seq_count = seq_lengths.shape[0]
    seq_index = jnp.arange(seq_count, dtype=jnp.int32)
    is_mine = seq_owner == device
    first_seq = jnp.min(jnp.where(is_mine, seq_index, seq_count))
    second_seq = jnp.min(jnp.where(is_mine & (seq_index != first_seq), seq_index, seq_count))
    len_first = jnp.sum(jnp.where(seq_index == first_seq, seq_lengths, 0))
    len_second = jnp.sum(jnp.where(seq_index == second_seq, seq_lengths, 0))
    row_index = jnp.arange(row_count, dtype=jnp.int32)
    segment = (row_index >= len_first).astype(jnp.int32) + (
        row_index >= len_first + len_second
    ).astype(jnp.int32)
    seg_start = jnp.where(
        segment == 0, 0, jnp.where(segment == 1, len_first, len_first + len_second)
    )
    position = row_index - seg_start
    row_valid = (segment < 2).astype(jnp.float32)
    allowed = (segment[:, None] == segment[None, :]) & (row_index[None, :] <= row_index[:, None])
    return (position, row_valid, allowed)


def rope_tables(position, head_size):
    half_size = head_size // 2
    frequency = ROPE_BASE ** (-jnp.arange(half_size, dtype=jnp.float32) * 2.0 / head_size)
    angles = position.astype(jnp.float32)[:, None] * frequency[None, :]
    return (jnp.cos(angles), jnp.sin(angles))


def rotate(values, cosine, sine_table):
    half_size = values.shape[-1] // 2
    front_half = values[..., :half_size]
    back_half = values[..., half_size:]
    cos_part = cosine[:, None, :]
    sin_part = sine_table[:, None, :]
    return jnp.concatenate(
        [
            front_half * cos_part - back_half * sin_part,
            back_half * cos_part + front_half * sin_part,
        ],
        axis=-1,
    )


def unrotate(gradient, cosine, sine_table):
    half_size = gradient.shape[-1] // 2
    front_half = gradient[..., :half_size]
    back_half = gradient[..., half_size:]
    cos_part = cosine[:, None, :]
    sin_part = sine_table[:, None, :]
    return jnp.concatenate(
        [
            front_half * cos_part + back_half * sin_part,
            back_half * cos_part - front_half * sin_part,
        ],
        axis=-1,
    )


def rms_scale(values):
    return lax.rsqrt(jnp.mean(values * values, axis=-1, keepdims=True) + EPSILON)


def outer_sum(left_side, right_side):
    return lax.dot_general(
        left_side, right_side, (((0,), (0,)), ((), ())), preferred_element_type=jnp.float32
    )


def times_t(left_side, right_side):
    return lax.dot_general(
        left_side, right_side, (((1,), (1,)), ((), ())), preferred_element_type=jnp.float32
    )


def pack_shards(shard_list):
    return jnp.concatenate([piece.reshape(1, -1) for piece in shard_list], axis=1)


def unpack_gathered(whole, shard_list):
    result_list = []
    offset = 0
    for piece in shard_list:
        width = piece.shape[0]
        result_list.append(whole[:, offset : offset + width].reshape(-1))
        offset = offset + width
    return result_list


def pack_grads(grad_list, count):
    return jnp.concatenate([item.reshape(count, -1) for item in grad_list], axis=1)


def unpack_grads(summed, grad_list, count):
    result_list = []
    offset = 0
    for item in grad_list:
        width = item.size // count
        result_list.append(summed[:, offset : offset + width].reshape(-1))
        offset = offset + width
    return result_list


def shape_weights(flat_list):
    query_flat, key_flat, value_flat, out_flat, gate_flat, up_flat, down_flat = flat_list
    return (
        query_flat.reshape(D, HEADS * HD),
        key_flat.reshape(D, KV_HEADS * HD),
        value_flat.reshape(D, KV_HEADS * HD),
        out_flat.reshape(HEADS * HD, D),
        gate_flat.reshape(D, FF),
        up_flat.reshape(D, FF),
        down_flat.reshape(FF, D),
    )


def on_device(
    tokens,
    cotangent,
    seq_lengths,
    seq_owner,
    query_weight,
    key_weight,
    value_weight,
    out_weight,
    gate_weight,
    up_weight,
    down_weight,
    attention_gain,
    feedforward_gain,
):
    row_count = tokens.shape[0]
    groups = HEADS // KV_HEADS
    score_scale = 1.0 / math.sqrt(HD)
    count = lax.axis_size("fsdp")
    device = lax.axis_index("fsdp")
    position, row_valid, allowed = own_rows(seq_lengths, seq_owner, device, row_count)
    cosine, sine_table = rope_tables(position, HD)
    shard_list = (
        query_weight,
        key_weight,
        value_weight,
        out_weight,
        gate_weight,
        up_weight,
        down_weight,
    )
    gathered = lax.all_gather(pack_shards(shard_list), "fsdp", axis=0, tiled=True)
    w_query, w_key, w_value, w_out, w_gate, w_up, w_down = shape_weights(
        unpack_gathered(gathered, shard_list)
    )
    inputs = tokens.astype(jnp.float32)
    scale_one = rms_scale(inputs)
    normed_one = inputs * scale_one
    low_one = (normed_one * attention_gain).astype(jnp.bfloat16)
    query_pre = jnp.dot(low_one, w_query, preferred_element_type=jnp.float32).reshape(
        row_count, HEADS, HD
    )
    key_pre = jnp.dot(low_one, w_key, preferred_element_type=jnp.float32).reshape(
        row_count, KV_HEADS, HD
    )
    value_low = (
        jnp.dot(low_one, w_value, preferred_element_type=jnp.float32)
        .astype(jnp.bfloat16)
        .reshape(row_count, KV_HEADS, HD)
    )
    query_low = (
        rotate(query_pre, cosine, sine_table)
        .astype(jnp.bfloat16)
        .reshape(row_count, KV_HEADS, groups, HD)
    )
    key_low = rotate(key_pre, cosine, sine_table).astype(jnp.bfloat16)
    scores = (
        jnp.einsum("ikgd,jkd->kgij", query_low, key_low, preferred_element_type=jnp.float32)
        * score_scale
    )
    masked = jnp.where(allowed[None, None], scores, MASKED_SCORE)
    row_max = jnp.max(masked, axis=-1, keepdims=True)
    exp_scores = jnp.exp(masked - row_max)
    row_total = jnp.sum(exp_scores, axis=-1, keepdims=True)
    log_total = row_max + jnp.log(row_total)
    prob_rows = (exp_scores / row_total).astype(jnp.bfloat16)
    attended = jnp.einsum(
        "kgij,jkd->ikgd", prob_rows, value_low, preferred_element_type=jnp.float32
    )
    attended_low = attended.reshape(row_count, HEADS * HD).astype(jnp.bfloat16)
    middle = inputs + jnp.dot(attended_low, w_out, preferred_element_type=jnp.float32)
    scale_two = rms_scale(middle)
    normed_two = middle * scale_two
    low_two = (normed_two * feedforward_gain).astype(jnp.bfloat16)
    gate_pre = jnp.dot(low_two, w_gate, preferred_element_type=jnp.float32)
    upward = jnp.dot(low_two, w_up, preferred_element_type=jnp.float32)
    sigmoid_gate = jax.nn.sigmoid(gate_pre)
    silu_gate = gate_pre * sigmoid_gate
    hidden_low = (silu_gate * upward).astype(jnp.bfloat16)
    branch_two = jnp.dot(hidden_low, w_down, preferred_element_type=jnp.float32)
    layer_out = (row_valid[:, None] * (middle + branch_two)).astype(jnp.bfloat16)
    grad_out = row_valid[:, None] * cotangent.astype(jnp.float32)
    grad_out_low = grad_out.astype(jnp.bfloat16)
    grad_wdown = outer_sum(hidden_low, grad_out_low)
    grad_hidden = times_t(grad_out_low, w_down).astype(jnp.bfloat16).astype(jnp.float32)
    grad_up = (grad_hidden * silu_gate).astype(jnp.bfloat16)
    grad_gate = (
        grad_hidden * upward * sigmoid_gate * (1.0 + gate_pre * (1.0 - sigmoid_gate))
    ).astype(jnp.bfloat16)
    grad_wgate = outer_sum(low_two, grad_gate)
    grad_wup = outer_sum(low_two, grad_up)
    grad_norm_two = times_t(grad_gate, w_gate) + times_t(grad_up, w_up)
    grad_gain_two = jnp.sum(grad_norm_two * normed_two, axis=0)
    scaled_two = grad_norm_two * feedforward_gain
    grad_middle = grad_out + scale_two * (
        scaled_two - normed_two * jnp.mean(scaled_two * normed_two, axis=-1, keepdims=True)
    )
    grad_branch_low = grad_middle.astype(jnp.bfloat16)
    grad_wout = outer_sum(attended_low, grad_branch_low)
    grad_attended = (
        times_t(grad_branch_low, w_out)
        .astype(jnp.bfloat16)
        .reshape(row_count, KV_HEADS, groups, HD)
    )
    scores_again = (
        jnp.einsum("ikgd,jkd->kgij", query_low, key_low, preferred_element_type=jnp.float32)
        * score_scale
    )
    probs_again = jnp.exp(jnp.where(allowed[None, None], scores_again, MASKED_SCORE) - log_total)
    grad_value = jnp.einsum(
        "kgij,ikgd->jkd",
        probs_again.astype(jnp.bfloat16),
        grad_attended,
        preferred_element_type=jnp.float32,
    )
    grad_probs = jnp.einsum(
        "ikgd,jkd->kgij", grad_attended, value_low, preferred_element_type=jnp.float32
    )
    inner_sum = jnp.sum(probs_again * grad_probs, axis=-1, keepdims=True)
    grad_scores = (probs_again * (grad_probs - inner_sum)).astype(jnp.bfloat16)
    grad_query = (
        jnp.einsum("kgij,jkd->ikgd", grad_scores, key_low, preferred_element_type=jnp.float32)
        * score_scale
    )
    grad_key = (
        jnp.einsum("kgij,ikgd->jkd", grad_scores, query_low, preferred_element_type=jnp.float32)
        * score_scale
    )
    grad_query_low = (
        unrotate(grad_query.reshape(row_count, HEADS, HD), cosine, sine_table)
        .reshape(row_count, HEADS * HD)
        .astype(jnp.bfloat16)
    )
    grad_key_low = (
        unrotate(grad_key, cosine, sine_table)
        .reshape(row_count, KV_HEADS * HD)
        .astype(jnp.bfloat16)
    )
    grad_value_low = grad_value.reshape(row_count, KV_HEADS * HD).astype(jnp.bfloat16)
    grad_wquery = outer_sum(low_one, grad_query_low)
    grad_wkey = outer_sum(low_one, grad_key_low)
    grad_wvalue = outer_sum(low_one, grad_value_low)
    grad_norm_one = (
        times_t(grad_query_low, w_query)
        + times_t(grad_key_low, w_key)
        + times_t(grad_value_low, w_value)
    )
    grad_gain_one = jnp.sum(grad_norm_one * normed_one, axis=0)
    scaled_one = grad_norm_one * attention_gain
    grad_inputs = grad_middle + scale_one * (
        scaled_one - normed_one * jnp.mean(scaled_one * normed_one, axis=-1, keepdims=True)
    )
    gain_one_sum, gain_two_sum = lax.psum((grad_gain_one, grad_gain_two), "fsdp")
    every_list = (grad_wquery, grad_wkey, grad_wvalue, grad_wout, grad_wgate, grad_wup, grad_wdown)
    every_summed = lax.psum_scatter(
        pack_grads(every_list, count), "fsdp", scatter_dimension=0, tiled=True
    )
    query_shard, key_shard, value_shard, out_shard, gate_shard, up_shard, down_shard = unpack_grads(
        every_summed, every_list, count
    )
    return (
        layer_out,
        grad_inputs.astype(jnp.bfloat16),
        query_shard,
        key_shard,
        value_shard,
        out_shard,
        gate_shard,
        up_shard,
        down_shard,
        gain_one_sum,
        gain_two_sum,
    )


BLOCK = 32
LINE = 4
CHIPS = 16
MESH = pl.DeviceIdType.MESH


def chip_place():
    device = lax.axis_index("fsdp")
    core, chip = device % 2, device // 2
    return core, chip // 4, (chip // 2) % 2, chip % 2


def chip_number(z, y, x):
    return (z * 2 + y) * 2 + x


def greet_neighbours(core, z, y, x):
    barrier = pltpu.get_barrier_semaphore()

    def greet(z_to, y_to, x_to):
        pl.semaphore_signal(
            barrier,
            inc=1,
            device_id=(chip_number(z_to, y_to, x_to) * 2 + core,),
            device_id_type=MESH,
        )

    greet(z, 1 - y, x)
    greet(z, y, 1 - x)

    @pl.when(z > 0)
    def _():
        greet(z - 1, y, x)

    @pl.when(z < LINE - 1)
    def _():
        greet(z + 1, y, x)

    pl.semaphore_wait(barrier, jnp.where((z > 0) & (z < LINE - 1), 4, 3))


def half_rows(refs, half):
    result = []
    for ref in refs:
        rows = ref.shape[-2]
        first = (rows // 2 + 15) // 16 * 16
        result.append(pl.ds(0, first) if half == 0 else pl.ds(first, rows - first))
    return result


def steps_at(distance):
    return (0,) if distance == 0 else (-distance, distance)


def gather_kernel(*refs):
    ins, outs = refs[0:3], refs[3:6]
    own_sem, recv_sem, up_sem, down_sem, first_sem, second_sem = refs[6:]
    core, z, y, x = chip_place()
    greet_neighbours(core, z, y, x)
    me = chip_number(z, y, x)
    rows = [half_rows(ins, half) for half in range(2)]
    pending = []

    def send(half, source, is_own, sem, slot, target):
        for i in range(3):
            span = rows[half][i]
            src = ins[i].at[span] if is_own else outs[i].at[source, span]
            copy = pltpu.make_async_remote_copy(
                src_ref=src,
                dst_ref=outs[i].at[source, span],
                send_sem=sem.at[half, i, slot],
                recv_sem=recv_sem.at[half, i, source],
                device_id=(target * 2 + core,),
                device_id_type=MESH,
            )
            copy.start()
            yield copy

    def send_all(condition, *args):
        def run():
            for _ in send(*args):
                pass

        if condition is None:
            run()
        else:
            pl.when(condition)(run)
        pending.append((condition, args))

    def receive(half, source):
        for i in range(3):
            view = outs[i].at[source, rows[half][i]]
            pltpu.make_async_remote_copy(
                src_ref=view,
                dst_ref=view,
                send_sem=own_sem.at[i],
                recv_sem=recv_sem.at[half, i, source],
                device_id=(me * 2 + core,),
                device_id_type=MESH,
            ).wait_recv()

    def across(half, place):
        return (1 - y, x) if (half == 0) == (place == 0) else (y, 1 - x)

    def inside(step):
        return (z + step >= 0) & (z + step < LINE)

    def spread_line(half, step):
        z_from = z + step
        source = chip_number(z_from, y, x)
        own = step == 0
        ok = None if own else inside(step)
        if step >= 0:
            cond = z > 0 if own else (ok & (z > 0))
            send_all(cond, half, source, own, down_sem, z_from, chip_number(z - 1, y, x))
        if step <= 0:
            cond = z < LINE - 1 if own else (ok & (z < LINE - 1))
            send_all(cond, half, source, own, up_sem, z_from, chip_number(z + 1, y, x))
        send_all(ok, half, source, own, first_sem, z_from, chip_number(z, *across(half, 0)))
        send_all(ok, half, source, own, second_sem, z_from, chip_number(z, *across(half, 1)))

    def spread_side(half, step):
        z_from = z + step
        source = chip_number(z_from, *across(half, 0))
        ok = None if step == 0 else inside(step)
        if ok is None:
            receive(half, source)
        else:
            pl.when(ok)(lambda: receive(half, source))
        send_all(
            ok, half, source, False, second_sem, LINE + z_from, chip_number(z, *across(half, 1))
        )

    local = [pltpu.make_async_copy(ins[i], outs[i].at[me], own_sem.at[i]) for i in range(3)]
    for half in range(2):
        spread_line(half, 0)
    for copy in local:
        copy.start()
    for distance in range(LINE):
        if distance > 0:
            for half in range(2):
                for step in steps_at(distance):
                    pl.when(inside(step))(
                        lambda: receive(half, chip_number(z + step, y, x))
                    )
                    spread_line(half, step)
        for half in range(2):
            for step in steps_at(distance):
                spread_side(half, step)
    for half in range(2):
        y_far, x_far = across(half, 1)
        for z_from in range(LINE):
            receive(half, chip_number(z_from, y_far, x_far))
            receive(half, chip_number(z_from, 1 - y, 1 - x))
    for copy in local:
        copy.wait()
    for condition, (half, source, is_own, sem, slot, target) in pending:

        def finish():
            for i in range(3):
                span = rows[half][i]
                src = ins[i].at[span] if is_own else outs[i].at[source, span]
                pltpu.make_async_remote_copy(
                    src_ref=src,
                    dst_ref=outs[i].at[source, span],
                    send_sem=sem.at[half, i, slot],
                    recv_sem=recv_sem.at[half, i, source],
                    device_id=(target * 2 + core,),
                    device_id_type=MESH,
                ).wait_send()

        if condition is None:
            finish()
        else:
            pl.when(condition)(finish)


def gather_chips(blocks):
    dma = pltpu.SemaphoreType.DMA
    return pl.pallas_call(
        gather_kernel,
        out_shape=[jax.ShapeDtypeStruct((CHIPS,) + item.shape, item.dtype) for item in blocks],
        in_specs=[pl.BlockSpec(memory_space=pl.ANY)] * 3,
        out_specs=[pl.BlockSpec(memory_space=pl.ANY)] * 3,
        scratch_shapes=[
            dma((3,)),
            dma((2, 3, CHIPS)),
            dma((2, 3, LINE)),
            dma((2, 3, LINE)),
            dma((2, 3, LINE)),
            dma((2, 3, 2 * LINE)),
        ],
        compiler_params=pltpu.CompilerParams(collective_id=1, has_side_effects=True),
        name="gather_chips",
    )(*blocks)


def scatter_kernel(*refs):
    ins, outs = refs[0:3], refs[3:6]
    far, side, low, high = refs[6:9], refs[9:12], refs[12:15], refs[15:18]
    far_send, far_recv, side_send, side_recv, up_send, low_recv, down_send, high_recv = refs[18:]
    core, z, y, x = chip_place()
    greet_neighbours(core, z, y, x)
    rows = [half_rows(outs, half) for half in range(2)]
    pending = []

    def across(half, place):
        return (1 - y, x) if (half == 0) == (place == 0) else (y, 1 - x)

    def inside(step):
        return (z + step >= 0) & (z + step < LINE)

    def copies(half, source, source_at, buffer, slot, send_sem, recv_sem, target):
        return [
            pltpu.make_async_remote_copy(
                src_ref=source[i].at[source_at, rows[half][i]],
                dst_ref=buffer[i].at[slot, rows[half][i]],
                send_sem=send_sem.at[half, i, slot],
                recv_sem=recv_sem.at[half, i, slot],
                device_id=(target * 2 + core,),
                device_id_type=MESH,
            )
            for i in range(3)
        ]

    def send(condition, *args):
        def run():
            for copy in copies(*args):
                copy.start()

        pl.when(condition)(run)
        pending.append((condition, args))

    def receive(half, buffer, slot, send_sem, recv_sem):
        for copy in copies(half, buffer, slot, buffer, slot, send_sem, recv_sem, 0):
            copy.wait_recv()

    def add(half, result, result_at, *terms):
        for i in range(3):
            span = rows[half][i]
            total = None
            for buffer, slot in terms:
                value = buffer[i][slot, span, :].astype(jnp.float32)
                total = value if total is None else total + value
            if result_at is None:
                result[i][span, :] = total.astype(jnp.bfloat16)
            else:
                result[i][result_at, span, :] = total.astype(jnp.bfloat16)

    def over_side(half, step):
        z_to = z + step
        place = across(half, 0)

        def work():
            receive(half, far, LINE + z_to, far_send, far_recv)
            add(half, far, LINE + z_to, (far, LINE + z_to), (ins, chip_number(z_to, *place)))

        pl.when(inside(step))(work)
        send(
            inside(step), half, far, LINE + z_to, side, z_to, side_send, side_recv, chip_number(z, *place)
        )

    def over_line(half, step):
        z_to = z + step

        def work():
            receive(half, far, z_to, far_send, far_recv)
            receive(half, side, z_to, side_send, side_recv)
            add(
                half, side, z_to, (side, z_to), (far, z_to), (ins, chip_number(z_to, y, x))
            )
            if step >= 0:

                @pl.when(z > 0)
                def _():
                    receive(half, low, z_to, up_send, low_recv)
                    add(half, side, z_to, (side, z_to), (low, z_to))

            if step <= 0:

                @pl.when(z < LINE - 1)
                def _():
                    receive(half, high, z_to, down_send, high_recv)
                    add(half, side, z_to, (side, z_to), (high, z_to))

            if step == 0:
                add(half, outs, None, (side, z_to))

        pl.when(inside(step))(work)
        if step > 0:
            send(
                inside(step), half, side, z_to, low, z_to, up_send, low_recv, chip_number(z + 1, y, x)
            )
        if step < 0:
            send(
                inside(step), half, side, z_to, high, z_to, down_send, high_recv, chip_number(z - 1, y, x)
            )

    for distance in reversed(range(LINE)):
        for step in steps_at(distance):
            for half in range(2):
                y_to, x_to = across(half, 1)
                target = chip_number(z, y_to, x_to)
                z_to = z + step
                first = chip_number(z_to, 1 - y, 1 - x)
                own = chip_number(z_to, y_to, x_to)
                ok = inside(step)
                send(ok, half, ins, first, far, LINE + z_to, far_send, far_recv, target)
                send(ok, half, ins, own, far, z_to, far_send, far_recv, target)
    for distance in (3, 2, 1, 0, -1):
        if distance >= 0:
            for step in steps_at(distance):
                for half in range(2):
                    over_side(half, step)
        if distance < LINE - 1:
            for step in steps_at(distance + 1):
                for half in range(2):
                    over_line(half, step)
    for condition, args in pending:

        def finish():
            for copy in copies(*args):
                copy.wait_send()

        pl.when(condition)(finish)


def scatter_chips(blocks):
    dma = pltpu.SemaphoreType.DMA

    def slots(number):
        return [pltpu.VMEM((number,) + item.shape[1:], item.dtype) for item in blocks]

    return pl.pallas_call(
        scatter_kernel,
        out_shape=[jax.ShapeDtypeStruct(item.shape[1:], item.dtype) for item in blocks],
        in_specs=[pl.BlockSpec(memory_space=pltpu.VMEM)] * 3,
        out_specs=[pl.BlockSpec(memory_space=pltpu.VMEM)] * 3,
        scratch_shapes=slots(2 * LINE)
        + slots(LINE)
        + slots(LINE)
        + slots(LINE)
        + [dma((2, 3, 2 * LINE))] * 2
        + [dma((2, 3, LINE))] * 6,
        compiler_params=pltpu.CompilerParams(
            collective_id=2, has_side_effects=True, vmem_limit_bytes=44 * 1024 * 1024
        ),
        name="scatter_chips",
    )(*blocks)


def pad_rows(block, spare):
    return jnp.pad(block, ((0, spare), (0, 0)))


def spread(values, count):
    rows = values.shape[0]
    wide = values.reshape(rows, count, -1)
    return jnp.pad(wide, ((0, 0), (0, 0), (0, BLOCK - wide.shape[2]))).reshape(rows, count * BLOCK)


def gather_in(values, count, width):
    rows = values.shape[0]
    return values.reshape(rows, count, BLOCK)[:, :, :width].reshape(rows, count * width)


def paired_on_device(
    tokens,
    cotangent,
    seq_lengths,
    seq_owner,
    query_weight,
    key_weight,
    value_weight,
    out_weight,
    gate_weight,
    up_weight,
    down_weight,
    attention_gain,
    feedforward_gain,
):
    row_count = tokens.shape[0]
    groups = HEADS // KV_HEADS
    score_scale = 1.0 / math.sqrt(HD)
    count = lax.axis_size("fsdp")
    chips = count // 2
    width = D // count
    units = FF // count
    spare = BLOCK - width
    device = lax.axis_index("fsdp")
    core = device % 2
    swap = [(i, i ^ 1) for i in range(count)]

    def other_core(values):
        return lax.ppermute(values, "fsdp", swap)

    def in_core_order(mine, theirs, axis):
        return jnp.where(
            core == 0,
            jnp.concatenate([mine, theirs], axis=axis),
            jnp.concatenate([theirs, mine], axis=axis),
        )

    def take_core(pair, index):
        return lax.dynamic_index_in_dim(pair, index, axis=0, keepdims=False)

    attention_shard = pad_rows(
        jnp.concatenate(
            [
                query_weight.reshape(width, HEADS * HD),
                key_weight.reshape(width, KV_HEADS * HD),
                value_weight.reshape(width, KV_HEADS * HD),
                out_weight.reshape(width, D),
            ],
            axis=1,
        ),
        spare,
    )
    gate_up = jnp.stack([gate_weight.reshape(width, chips, 2, units), up_weight.reshape(width, chips, 2, units)])
    gate_up = gate_up.transpose(3, 0, 1, 2, 4).reshape(2, 2, width, chips * units)
    gate_up = jnp.pad(gate_up, ((0, 0), (0, 0), (0, spare), (0, 0)))
    gate_up_other = other_core(take_core(gate_up, 1 - core))
    gate_up_pair = in_core_order(take_core(gate_up, core), gate_up_other, 1)
    attention_mine, gate_up_all, down_all = gather_chips(
        [
            attention_shard,
            gate_up_pair.reshape(4 * BLOCK, chips * units),
            down_weight.reshape(units, D),
        ]
    )
    attention_other = other_core(attention_mine)
    w_gate = gate_up_all[:, : 2 * BLOCK].reshape(count * BLOCK, chips * units)
    w_up = gate_up_all[:, 2 * BLOCK :].reshape(count * BLOCK, chips * units)
    w_down = down_all.reshape(chips * units, D)

    attention_all = in_core_order(attention_mine[:, None], attention_other[:, None], 1).reshape(
        count * BLOCK, 2 * HEADS * HD + 2 * KV_HEADS * HD
    )
    wide_qkv = (HEADS + 2 * KV_HEADS) * HD
    w_qkv = attention_all[:, :wide_qkv]
    w_out = attention_all[:, wide_qkv:]

    position, row_valid, allowed = own_rows(seq_lengths, seq_owner, device, row_count)
    cosine, sine_table = rope_tables(position, HD)
    grad_out = row_valid[:, None] * cotangent.astype(jnp.float32)
    grad_out_low = grad_out.astype(jnp.bfloat16)
    grad_out_both = jnp.concatenate([grad_out_low, other_core(grad_out_low)], axis=0)

    inputs = tokens.astype(jnp.float32)
    scale_one = rms_scale(inputs)
    normed_one = inputs * scale_one
    low_one = spread((normed_one * attention_gain).astype(jnp.bfloat16), count)
    qkv = jnp.dot(low_one, w_qkv, preferred_element_type=jnp.float32)
    query_pre = qkv[:, : HEADS * HD].reshape(row_count, HEADS, HD)
    key_pre = qkv[:, HEADS * HD : (HEADS + KV_HEADS) * HD].reshape(row_count, KV_HEADS, HD)
    value_low = qkv[:, (HEADS + KV_HEADS) * HD :].astype(jnp.bfloat16).reshape(row_count, KV_HEADS, HD)
    query_low = (
        rotate(query_pre, cosine, sine_table)
        .astype(jnp.bfloat16)
        .reshape(row_count, KV_HEADS, groups, HD)
    )
    key_low = rotate(key_pre, cosine, sine_table).astype(jnp.bfloat16)
    scores = (
        jnp.einsum("ikgd,jkd->kgij", query_low, key_low, preferred_element_type=jnp.float32)
        * score_scale
    )
    masked = jnp.where(allowed[None, None], scores, MASKED_SCORE)
    row_max = jnp.max(masked, axis=-1, keepdims=True)
    exp_scores = jnp.exp(masked - row_max)
    row_total = jnp.sum(exp_scores, axis=-1, keepdims=True)
    probs = exp_scores / row_total
    prob_rows = probs.astype(jnp.bfloat16)
    attended = jnp.einsum(
        "kgij,jkd->ikgd", prob_rows, value_low, preferred_element_type=jnp.float32
    )
    attended_low = spread(attended.reshape(row_count, HEADS * HD).astype(jnp.bfloat16), count)
    middle = inputs + jnp.dot(attended_low, w_out, preferred_element_type=jnp.float32)
    scale_two = rms_scale(middle)
    normed_two = middle * scale_two
    low_two = spread((normed_two * feedforward_gain).astype(jnp.bfloat16), count)
    low_two_both = jnp.concatenate([low_two, other_core(low_two)], axis=0)

    gate_pre = jnp.dot(low_two_both, w_gate, preferred_element_type=jnp.float32)
    upward = jnp.dot(low_two_both, w_up, preferred_element_type=jnp.float32)
    sigmoid_gate = jax.nn.sigmoid(gate_pre)
    silu_gate = gate_pre * sigmoid_gate
    hidden_low = (silu_gate * upward).astype(jnp.bfloat16)
    branch_both = jnp.dot(hidden_low, w_down, preferred_element_type=jnp.float32)
    branch_two = branch_both[:row_count] + other_core(branch_both[row_count:])
    layer_out = (row_valid[:, None] * (middle + branch_two)).astype(jnp.bfloat16)

    grad_wdown = outer_sum(hidden_low, grad_out_both).astype(jnp.bfloat16)
    grad_hidden = times_t(grad_out_both, w_down).astype(jnp.bfloat16).astype(jnp.float32)
    grad_up = (grad_hidden * silu_gate).astype(jnp.bfloat16)
    grad_gate = (
        grad_hidden * upward * sigmoid_gate * (1.0 + gate_pre * (1.0 - sigmoid_gate))
    ).astype(jnp.bfloat16)
    grad_wgate = outer_sum(low_two_both, grad_gate).astype(jnp.bfloat16)
    grad_wup = outer_sum(low_two_both, grad_up).astype(jnp.bfloat16)
    grad_gate_up = jnp.concatenate(
        [
            grad_wgate.reshape(chips, 2 * BLOCK, chips * units),
            grad_wup.reshape(chips, 2 * BLOCK, chips * units),
        ],
        axis=1,
    )
    grad_norm_both = times_t(grad_gate, w_gate) + times_t(grad_up, w_up)
    grad_norm_two = gather_in(
        grad_norm_both[:row_count] + other_core(grad_norm_both[row_count:]), count, width
    )
    grad_gain_two = jnp.sum(grad_norm_two * normed_two, axis=0)
    scaled_two = grad_norm_two * feedforward_gain
    grad_middle = grad_out + scale_two * (
        scaled_two - normed_two * jnp.mean(scaled_two * normed_two, axis=-1, keepdims=True)
    )
    grad_branch_low = grad_middle.astype(jnp.bfloat16)
    grad_wout = outer_sum(attended_low, grad_branch_low)
    grad_attended = gather_in(
        times_t(grad_branch_low, w_out).astype(jnp.bfloat16), count, width
    ).reshape(row_count, KV_HEADS, groups, HD)
    grad_value = jnp.einsum(
        "kgij,ikgd->jkd", prob_rows, grad_attended, preferred_element_type=jnp.float32
    )
    grad_probs = jnp.einsum(
        "ikgd,jkd->kgij", grad_attended, value_low, preferred_element_type=jnp.float32
    )
    inner_sum = jnp.sum(probs * grad_probs, axis=-1, keepdims=True)
    grad_scores = (probs * (grad_probs - inner_sum)).astype(jnp.bfloat16)
    grad_query = (
        jnp.einsum("kgij,jkd->ikgd", grad_scores, key_low, preferred_element_type=jnp.float32)
        * score_scale
    )
    grad_key = (
        jnp.einsum("kgij,ikgd->jkd", grad_scores, query_low, preferred_element_type=jnp.float32)
        * score_scale
    )
    grad_qkv = jnp.concatenate(
        [
            unrotate(grad_query.reshape(row_count, HEADS, HD), cosine, sine_table)
            .reshape(row_count, HEADS * HD)
            .astype(jnp.bfloat16),
            unrotate(grad_key, cosine, sine_table)
            .reshape(row_count, KV_HEADS * HD)
            .astype(jnp.bfloat16),
            grad_value.reshape(row_count, KV_HEADS * HD).astype(jnp.bfloat16),
        ],
        axis=1,
    )
    grad_wqkv = outer_sum(low_one, grad_qkv)
    grad_attention = jnp.concatenate([grad_wqkv, grad_wout], axis=1).reshape(
        chips, 2, BLOCK, 2 * HEADS * HD + 2 * KV_HEADS * HD
    )
    keep = lax.dynamic_index_in_dim(grad_attention, core, axis=1, keepdims=False)
    give = lax.dynamic_index_in_dim(grad_attention, 1 - core, axis=1, keepdims=False)
    attention_sum, gate_up_sum, down_sum = scatter_chips(
        [
            (keep + other_core(give.astype(jnp.bfloat16)).astype(jnp.float32)).astype(jnp.bfloat16),
            grad_gate_up,
            grad_wdown.reshape(chips, units, D),
        ]
    )
    attention_sum = attention_sum[:width].astype(jnp.float32)

    grad_norm_one = gather_in(times_t(grad_qkv, w_qkv), count, width)
    grad_gain_one = jnp.sum(grad_norm_one * normed_one, axis=0)
    scaled_one = grad_norm_one * attention_gain
    grad_inputs = grad_middle + scale_one * (
        scaled_one - normed_one * jnp.mean(scaled_one * normed_one, axis=-1, keepdims=True)
    )
    gain_sums = jnp.sum(
        lax.all_gather(jnp.stack([grad_gain_one, grad_gain_two]), "fsdp", axis=0), axis=0
    )

    gate_up_sum = gate_up_sum.reshape(2, 2, BLOCK, chips * units).transpose(1, 0, 2, 3)
    gate_up_got = other_core(take_core(gate_up_sum, 1 - core))
    gate_up_kept = take_core(gate_up_sum, core)
    halves = in_core_order(gate_up_kept[None], gate_up_got[None], 0)[:, :, :width]
    halves = halves.reshape(2, 2, width, chips, units).transpose(1, 2, 3, 0, 4).astype(jnp.float32)
    edge_key, edge_value = HEADS * HD, (HEADS + KV_HEADS) * HD
    return (
        layer_out,
        grad_inputs.astype(jnp.bfloat16),
        attention_sum[:, :edge_key].reshape(-1),
        attention_sum[:, edge_key:edge_value].reshape(-1),
        attention_sum[:, edge_value:wide_qkv].reshape(-1),
        attention_sum[:, wide_qkv:].reshape(-1),
        halves[0].reshape(-1),
        halves[1].reshape(-1),
        down_sum.astype(jnp.float32).reshape(-1),
        gain_sums[0],
        gain_sums[1],
    )


def solution(mesh):
    count = mesh.shape["fsdp"]
    whole_rows = count == 2 * CHIPS
    program = paired_on_device if whole_rows else on_device
    return jax.shard_map(
        program,
        mesh=mesh,
        in_specs=(
            P("fsdp", None),
            P("fsdp", None),
            P(),
            P(),
            P("fsdp"),
            P("fsdp"),
            P("fsdp"),
            P("fsdp"),
            P("fsdp"),
            P("fsdp"),
            P("fsdp"),
            P(),
            P(),
        ),
        out_specs=(
            P("fsdp", None),
            P("fsdp", None),
            P("fsdp"),
            P("fsdp"),
            P("fsdp"),
            P("fsdp"),
            P("fsdp"),
            P("fsdp"),
            P("fsdp"),
            P(),
            P(),
        ),
        check_vma=False,
    )
```

```python
import math

import jax
import jax.numpy as jnp
from jax import lax
from jax.experimental import pallas as pl
from jax.experimental.pallas import tpu as pltpu
from jax.sharding import PartitionSpec as P

D = 960
HEADS = 15
KV_HEADS = 5
HD = 64
FF = 2560


EPSILON = 1e-05
ROPE_BASE = 10000.0
MASKED_SCORE = -1e30


def own_rows(seq_lengths, seq_owner, device, row_count):
    seq_count = seq_lengths.shape[0]
    seq_index = jnp.arange(seq_count, dtype=jnp.int32)
    is_mine = seq_owner == device
    first_seq = jnp.min(jnp.where(is_mine, seq_index, seq_count))
    second_seq = jnp.min(jnp.where(is_mine & (seq_index != first_seq), seq_index, seq_count))
    len_first = jnp.sum(jnp.where(seq_index == first_seq, seq_lengths, 0))
    len_second = jnp.sum(jnp.where(seq_index == second_seq, seq_lengths, 0))
    row_index = jnp.arange(row_count, dtype=jnp.int32)
    segment = (row_index >= len_first).astype(jnp.int32) + (
        row_index >= len_first + len_second
    ).astype(jnp.int32)
    seg_start = jnp.where(
        segment == 0, 0, jnp.where(segment == 1, len_first, len_first + len_second)
    )
    position = row_index - seg_start
    row_valid = (segment < 2).astype(jnp.float32)
    allowed = (segment[:, None] == segment[None, :]) & (row_index[None, :] <= row_index[:, None])
    return (position, row_valid, allowed)


def rope_tables(position, head_size):
    half_size = head_size // 2
    frequency = ROPE_BASE ** (-jnp.arange(half_size, dtype=jnp.float32) * 2.0 / head_size)
    angles = position.astype(jnp.float32)[:, None] * frequency[None, :]
    return (jnp.cos(angles), jnp.sin(angles))


def rotate(values, cosine, sine_table):
    half_size = values.shape[-1] // 2
    front_half = values[..., :half_size]
    back_half = values[..., half_size:]
    cos_part = cosine[:, None, :]
    sin_part = sine_table[:, None, :]
    return jnp.concatenate(
        [
            front_half * cos_part - back_half * sin_part,
            back_half * cos_part + front_half * sin_part,
        ],
        axis=-1,
    )


def unrotate(gradient, cosine, sine_table):
    half_size = gradient.shape[-1] // 2
    front_half = gradient[..., :half_size]
    back_half = gradient[..., half_size:]
    cos_part = cosine[:, None, :]
    sin_part = sine_table[:, None, :]
    return jnp.concatenate(
        [
            front_half * cos_part + back_half * sin_part,
            back_half * cos_part - front_half * sin_part,
        ],
        axis=-1,
    )


def rms_scale(values):
    return lax.rsqrt(jnp.mean(values * values, axis=-1, keepdims=True) + EPSILON)


def outer_sum(left_side, right_side):
    return lax.dot_general(
        left_side, right_side, (((0,), (0,)), ((), ())), preferred_element_type=jnp.float32
    )


def times_t(left_side, right_side):
    return lax.dot_general(
        left_side, right_side, (((1,), (1,)), ((), ())), preferred_element_type=jnp.float32
    )


def pack_shards(shard_list):
    return jnp.concatenate([piece.reshape(1, -1) for piece in shard_list], axis=1)


def unpack_gathered(whole, shard_list):
    result_list = []
    offset = 0
    for piece in shard_list:
        width = piece.shape[0]
        result_list.append(whole[:, offset : offset + width].reshape(-1))
        offset = offset + width
    return result_list


def pack_grads(grad_list, count):
    return jnp.concatenate([item.reshape(count, -1) for item in grad_list], axis=1)


def unpack_grads(summed, grad_list, count):
    result_list = []
    offset = 0
    for item in grad_list:
        width = item.size // count
        result_list.append(summed[:, offset : offset + width].reshape(-1))
        offset = offset + width
    return result_list


def shape_weights(flat_list):
    query_flat, key_flat, value_flat, out_flat, gate_flat, up_flat, down_flat = flat_list
    return (
        query_flat.reshape(D, HEADS * HD),
        key_flat.reshape(D, KV_HEADS * HD),
        value_flat.reshape(D, KV_HEADS * HD),
        out_flat.reshape(HEADS * HD, D),
        gate_flat.reshape(D, FF),
        up_flat.reshape(D, FF),
        down_flat.reshape(FF, D),
    )


def on_device(
    tokens,
    cotangent,
    seq_lengths,
    seq_owner,
    query_weight,
    key_weight,
    value_weight,
    out_weight,
    gate_weight,
    up_weight,
    down_weight,
    attention_gain,
    feedforward_gain,
):
    row_count = tokens.shape[0]
    groups = HEADS // KV_HEADS
    score_scale = 1.0 / math.sqrt(HD)
    count = lax.axis_size("fsdp")
    device = lax.axis_index("fsdp")
    position, row_valid, allowed = own_rows(seq_lengths, seq_owner, device, row_count)
    cosine, sine_table = rope_tables(position, HD)
    shard_list = (
        query_weight,
        key_weight,
        value_weight,
        out_weight,
        gate_weight,
        up_weight,
        down_weight,
    )
    gathered = lax.all_gather(pack_shards(shard_list), "fsdp", axis=0, tiled=True)
    w_query, w_key, w_value, w_out, w_gate, w_up, w_down = shape_weights(
        unpack_gathered(gathered, shard_list)
    )
    inputs = tokens.astype(jnp.float32)
    scale_one = rms_scale(inputs)
    normed_one = inputs * scale_one
    low_one = (normed_one * attention_gain).astype(jnp.bfloat16)
    query_pre = jnp.dot(low_one, w_query, preferred_element_type=jnp.float32).reshape(
        row_count, HEADS, HD
    )
    key_pre = jnp.dot(low_one, w_key, preferred_element_type=jnp.float32).reshape(
        row_count, KV_HEADS, HD
    )
    value_low = (
        jnp.dot(low_one, w_value, preferred_element_type=jnp.float32)
        .astype(jnp.bfloat16)
        .reshape(row_count, KV_HEADS, HD)
    )
    query_low = (
        rotate(query_pre, cosine, sine_table)
        .astype(jnp.bfloat16)
        .reshape(row_count, KV_HEADS, groups, HD)
    )
    key_low = rotate(key_pre, cosine, sine_table).astype(jnp.bfloat16)
    scores = (
        jnp.einsum("ikgd,jkd->kgij", query_low, key_low, preferred_element_type=jnp.float32)
        * score_scale
    )
    masked = jnp.where(allowed[None, None], scores, MASKED_SCORE)
    row_max = jnp.max(masked, axis=-1, keepdims=True)
    exp_scores = jnp.exp(masked - row_max)
    row_total = jnp.sum(exp_scores, axis=-1, keepdims=True)
    log_total = row_max + jnp.log(row_total)
    prob_rows = (exp_scores / row_total).astype(jnp.bfloat16)
    attended = jnp.einsum(
        "kgij,jkd->ikgd", prob_rows, value_low, preferred_element_type=jnp.float32
    )
    attended_low = attended.reshape(row_count, HEADS * HD).astype(jnp.bfloat16)
    middle = inputs + jnp.dot(attended_low, w_out, preferred_element_type=jnp.float32)
    scale_two = rms_scale(middle)
    normed_two = middle * scale_two
    low_two = (normed_two * feedforward_gain).astype(jnp.bfloat16)
    gate_pre = jnp.dot(low_two, w_gate, preferred_element_type=jnp.float32)
    upward = jnp.dot(low_two, w_up, preferred_element_type=jnp.float32)
    sigmoid_gate = jax.nn.sigmoid(gate_pre)
    silu_gate = gate_pre * sigmoid_gate
    hidden_low = (silu_gate * upward).astype(jnp.bfloat16)
    branch_two = jnp.dot(hidden_low, w_down, preferred_element_type=jnp.float32)
    layer_out = (row_valid[:, None] * (middle + branch_two)).astype(jnp.bfloat16)
    grad_out = row_valid[:, None] * cotangent.astype(jnp.float32)
    grad_out_low = grad_out.astype(jnp.bfloat16)
    grad_wdown = outer_sum(hidden_low, grad_out_low)
    grad_hidden = times_t(grad_out_low, w_down).astype(jnp.bfloat16).astype(jnp.float32)
    grad_up = (grad_hidden * silu_gate).astype(jnp.bfloat16)
    grad_gate = (
        grad_hidden * upward * sigmoid_gate * (1.0 + gate_pre * (1.0 - sigmoid_gate))
    ).astype(jnp.bfloat16)
    grad_wgate = outer_sum(low_two, grad_gate)
    grad_wup = outer_sum(low_two, grad_up)
    grad_norm_two = times_t(grad_gate, w_gate) + times_t(grad_up, w_up)
    grad_gain_two = jnp.sum(grad_norm_two * normed_two, axis=0)
    scaled_two = grad_norm_two * feedforward_gain
    grad_middle = grad_out + scale_two * (
        scaled_two - normed_two * jnp.mean(scaled_two * normed_two, axis=-1, keepdims=True)
    )
    grad_branch_low = grad_middle.astype(jnp.bfloat16)
    grad_wout = outer_sum(attended_low, grad_branch_low)
    grad_attended = (
        times_t(grad_branch_low, w_out)
        .astype(jnp.bfloat16)
        .reshape(row_count, KV_HEADS, groups, HD)
    )
    scores_again = (
        jnp.einsum("ikgd,jkd->kgij", query_low, key_low, preferred_element_type=jnp.float32)
        * score_scale
    )
    probs_again = jnp.exp(jnp.where(allowed[None, None], scores_again, MASKED_SCORE) - log_total)
    grad_value = jnp.einsum(
        "kgij,ikgd->jkd",
        probs_again.astype(jnp.bfloat16),
        grad_attended,
        preferred_element_type=jnp.float32,
    )
    grad_probs = jnp.einsum(
        "ikgd,jkd->kgij", grad_attended, value_low, preferred_element_type=jnp.float32
    )
    inner_sum = jnp.sum(probs_again * grad_probs, axis=-1, keepdims=True)
    grad_scores = (probs_again * (grad_probs - inner_sum)).astype(jnp.bfloat16)
    grad_query = (
        jnp.einsum("kgij,jkd->ikgd", grad_scores, key_low, preferred_element_type=jnp.float32)
        * score_scale
    )
    grad_key = (
        jnp.einsum("kgij,ikgd->jkd", grad_scores, query_low, preferred_element_type=jnp.float32)
        * score_scale
    )
    grad_query_low = (
        unrotate(grad_query.reshape(row_count, HEADS, HD), cosine, sine_table)
        .reshape(row_count, HEADS * HD)
        .astype(jnp.bfloat16)
    )
    grad_key_low = (
        unrotate(grad_key, cosine, sine_table)
        .reshape(row_count, KV_HEADS * HD)
        .astype(jnp.bfloat16)
    )
    grad_value_low = grad_value.reshape(row_count, KV_HEADS * HD).astype(jnp.bfloat16)
    grad_wquery = outer_sum(low_one, grad_query_low)
    grad_wkey = outer_sum(low_one, grad_key_low)
    grad_wvalue = outer_sum(low_one, grad_value_low)
    grad_norm_one = (
        times_t(grad_query_low, w_query)
        + times_t(grad_key_low, w_key)
        + times_t(grad_value_low, w_value)
    )
    grad_gain_one = jnp.sum(grad_norm_one * normed_one, axis=0)
    scaled_one = grad_norm_one * attention_gain
    grad_inputs = grad_middle + scale_one * (
        scaled_one - normed_one * jnp.mean(scaled_one * normed_one, axis=-1, keepdims=True)
    )
    gain_one_sum, gain_two_sum = lax.psum((grad_gain_one, grad_gain_two), "fsdp")
    every_list = (grad_wquery, grad_wkey, grad_wvalue, grad_wout, grad_wgate, grad_wup, grad_wdown)
    every_summed = lax.psum_scatter(
        pack_grads(every_list, count), "fsdp", scatter_dimension=0, tiled=True
    )
    query_shard, key_shard, value_shard, out_shard, gate_shard, up_shard, down_shard = unpack_grads(
        every_summed, every_list, count
    )
    return (
        layer_out,
        grad_inputs.astype(jnp.bfloat16),
        query_shard,
        key_shard,
        value_shard,
        out_shard,
        gate_shard,
        up_shard,
        down_shard,
        gain_one_sum,
        gain_two_sum,
    )


BLOCK = 32
LINE = 4
CHIPS = 16
MESH = pl.DeviceIdType.MESH


def chip_place():
    device = lax.axis_index("fsdp")
    core, chip = device % 2, device // 2
    return core, chip // 4, (chip // 2) % 2, chip % 2


def chip_number(z, y, x):
    return (z * 2 + y) * 2 + x


def greet_neighbours(core, z, y, x):
    barrier = pltpu.get_barrier_semaphore()

    def greet(z_to, y_to, x_to, core_to=core):
        pl.semaphore_signal(
            barrier,
            inc=1,
            device_id=(chip_number(z_to, y_to, x_to) * 2 + core_to,),
            device_id_type=MESH,
        )

    greet(z, y, x, 1 - core)
    greet(z, 1 - y, x)
    greet(z, y, 1 - x)

    @pl.when(z > 0)
    def _():
        greet(z - 1, y, x)

    @pl.when(z < LINE - 1)
    def _():
        greet(z + 1, y, x)

    pl.semaphore_wait(barrier, jnp.where((z > 0) & (z < LINE - 1), 5, 4))


def half_rows(refs, half):
    result = []
    for ref in refs:
        rows = ref.shape[-2]
        first = (rows // 2 + 15) // 16 * 16
        result.append(pl.ds(0, first) if half == 0 else pl.ds(first, rows - first))
    return result


def steps_at(distance):
    return (0,) if distance == 0 else (-distance, distance)


def gather_kernel(*refs):
    ins, outs = refs[0:3], refs[3:6]
    own_sem, recv_sem, up_sem, down_sem, first_sem, second_sem, pair_send, pair_recv = refs[6:]
    core, z, y, x = chip_place()
    greet_neighbours(core, z, y, x)
    me = chip_number(z, y, x)
    rows = [half_rows(ins, half) for half in range(2)]
    pending = []

    def out_at(i, source, span, side=core):
        return outs[0].at[source, side, span] if i == 0 else outs[i].at[source, span]

    def to_pair(half, source, is_own):
        span = rows[half][0]
        return pltpu.make_async_remote_copy(
            src_ref=ins[0].at[span] if is_own else out_at(0, source, span),
            dst_ref=out_at(0, source, span),
            send_sem=pair_send.at[half, source],
            recv_sem=pair_recv.at[half, source],
            device_id=(me * 2 + 1 - core,),
            device_id_type=MESH,
        )

    def send(half, source, is_own, sem, slot, target):
        for i in range(3):
            span = rows[half][i]
            src = ins[i].at[span] if is_own else out_at(i, source, span)
            copy = pltpu.make_async_remote_copy(
                src_ref=src,
                dst_ref=out_at(i, source, span),
                send_sem=sem.at[half, i, slot],
                recv_sem=recv_sem.at[half, i, source],
                device_id=(target * 2 + core,),
                device_id_type=MESH,
            )
            copy.start()
            yield copy

    def send_all(condition, *args):
        def run():
            for _ in send(*args):
                pass

        if condition is None:
            run()
        else:
            pl.when(condition)(run)
        pending.append((condition, args))

    def receive(half, source):
        for i in range(3):
            view = out_at(i, source, rows[half][i])
            pltpu.make_async_remote_copy(
                src_ref=view,
                dst_ref=view,
                send_sem=own_sem.at[i],
                recv_sem=recv_sem.at[half, i, source],
                device_id=(me * 2 + 1 - core,),
                device_id_type=MESH,
            ).wait_recv()
        to_pair(half, source, False).start()

    def across(half, place):
        return (1 - y, x) if (half == 0) == (place == 0) else (y, 1 - x)

    def inside(step):
        return (z + step >= 0) & (z + step < LINE)

    def spread_line(half, step):
        z_from = z + step
        source = chip_number(z_from, y, x)
        own = step == 0
        ok = None if own else inside(step)
        if step >= 0:
            cond = z > 0 if own else (ok & (z > 0))
            send_all(cond, half, source, own, down_sem, z_from, chip_number(z - 1, y, x))
        if step <= 0:
            cond = z < LINE - 1 if own else (ok & (z < LINE - 1))
            send_all(cond, half, source, own, up_sem, z_from, chip_number(z + 1, y, x))
        send_all(ok, half, source, own, first_sem, z_from, chip_number(z, *across(half, 0)))
        send_all(ok, half, source, own, second_sem, z_from, chip_number(z, *across(half, 1)))

    def spread_side(half, step):
        z_from = z + step
        source = chip_number(z_from, *across(half, 0))
        ok = None if step == 0 else inside(step)
        if ok is None:
            receive(half, source)
        else:
            pl.when(ok)(lambda: receive(half, source))
        send_all(
            ok, half, source, False, second_sem, LINE + z_from, chip_number(z, *across(half, 1))
        )

    whole = [pl.ds(0, ref.shape[0]) for ref in ins]
    local = [
        pltpu.make_async_copy(ins[i], out_at(i, me, whole[i]), own_sem.at[i]) for i in range(3)
    ]
    for half in range(2):
        spread_line(half, 0)
        to_pair(half, me, True).start()
    for copy in local:
        copy.start()
    for distance in range(LINE):
        if distance > 0:
            for half in range(2):
                for step in steps_at(distance):
                    pl.when(inside(step))(
                        lambda: receive(half, chip_number(z + step, y, x))
                    )
                    spread_line(half, step)
        for half in range(2):
            for step in steps_at(distance):
                spread_side(half, step)
    for half in range(2):
        y_far, x_far = across(half, 1)
        for z_from in range(LINE):
            receive(half, chip_number(z_from, y_far, x_far))
            receive(half, chip_number(z_from, 1 - y, 1 - x))
    for copy in local:
        copy.wait()
    for half in range(2):
        span = rows[half][0]
        for source in range(CHIPS):
            view = out_at(0, source, span, 1 - core)
            pltpu.make_async_remote_copy(
                src_ref=view,
                dst_ref=view,
                send_sem=pair_send.at[half, source],
                recv_sem=pair_recv.at[half, source],
                device_id=(me * 2 + 1 - core,),
                device_id_type=MESH,
            ).wait_recv()
            to_pair(half, source, False).wait_send()
    for condition, (half, source, is_own, sem, slot, target) in pending:

        def finish():
            for i in range(3):
                span = rows[half][i]
                src = ins[i].at[span] if is_own else out_at(i, source, span)
                pltpu.make_async_remote_copy(
                    src_ref=src,
                    dst_ref=out_at(i, source, span),
                    send_sem=sem.at[half, i, slot],
                    recv_sem=recv_sem.at[half, i, source],
                    device_id=(target * 2 + core,),
                    device_id_type=MESH,
                ).wait_send()

        if condition is None:
            finish()
        else:
            pl.when(condition)(finish)


def gather_chips(blocks):
    dma = pltpu.SemaphoreType.DMA
    return pl.pallas_call(
        gather_kernel,
        out_shape=[
            jax.ShapeDtypeStruct((CHIPS,) + extra + item.shape, item.dtype)
            for item, extra in zip(blocks, ((2,), (), ()))
        ],
        in_specs=[pl.BlockSpec(memory_space=pl.ANY)] * 3,
        out_specs=[pl.BlockSpec(memory_space=pl.ANY)] * 3,
        scratch_shapes=[
            dma((3,)),
            dma((2, 3, CHIPS)),
            dma((2, 3, LINE)),
            dma((2, 3, LINE)),
            dma((2, 3, LINE)),
            dma((2, 3, 2 * LINE)),
            dma((2, CHIPS)),
            dma((2, CHIPS)),
        ],
        compiler_params=pltpu.CompilerParams(collective_id=1, has_side_effects=True),
        name="gather_chips",
    )(*blocks)


def scatter_kernel(*refs):
    ins, gains, outs, gains_out = refs[0:3], refs[3], refs[4:7], refs[7]
    far, side, low, high = refs[8:11], refs[11:14], refs[14:17], refs[17:20]
    far_send, far_recv, side_send, side_recv, up_send, low_recv, down_send, high_recv = refs[20:28]
    gain_sum, gain_got, gain_line, gain_send, gain_recv, line_up, line_down, line_recv = refs[28:]
    core, z, y, x = chip_place()
    greet_neighbours(core, z, y, x)
    rows = [half_rows(outs, half) for half in range(2)]
    pending = []

    def across(half, place):
        return (1 - y, x) if (half == 0) == (place == 0) else (y, 1 - x)

    def inside(step):
        return (z + step >= 0) & (z + step < LINE)

    def copies(half, source, source_at, buffer, slot, send_sem, recv_sem, target):
        return [
            pltpu.make_async_remote_copy(
                src_ref=source[i].at[source_at, rows[half][i]],
                dst_ref=buffer[i].at[slot, rows[half][i]],
                send_sem=send_sem.at[half, i, slot],
                recv_sem=recv_sem.at[half, i, slot],
                device_id=(target * 2 + core,),
                device_id_type=MESH,
            )
            for i in range(3)
        ]

    def send(condition, *args):
        def run():
            for copy in copies(*args):
                copy.start()

        pl.when(condition)(run)
        pending.append((condition, args))

    def receive(half, buffer, slot, send_sem, recv_sem):
        for copy in copies(half, buffer, slot, buffer, slot, send_sem, recv_sem, 0):
            copy.wait_recv()

    def add(half, result, result_at, *terms):
        for i in range(3):
            span = rows[half][i]
            total = None
            for buffer, slot in terms:
                value = buffer[i][slot, span, :].astype(jnp.float32)
                total = value if total is None else total + value
            if result_at is None:
                result[i][span, :] = total.astype(jnp.bfloat16)
            else:
                result[i][result_at, span, :] = total.astype(jnp.bfloat16)

    def over_side(half, step):
        z_to = z + step
        place = across(half, 0)

        def work():
            receive(half, far, LINE + z_to, far_send, far_recv)
            add(half, far, LINE + z_to, (far, LINE + z_to), (ins, chip_number(z_to, *place)))

        pl.when(inside(step))(work)
        send(
            inside(step), half, far, LINE + z_to, side, z_to, side_send, side_recv, chip_number(z, *place)
        )

    def over_line(half, step):
        z_to = z + step

        def work():
            receive(half, far, z_to, far_send, far_recv)
            receive(half, side, z_to, side_send, side_recv)
            add(
                half, side, z_to, (side, z_to), (far, z_to), (ins, chip_number(z_to, y, x))
            )
            if step >= 0:

                @pl.when(z > 0)
                def _():
                    receive(half, low, z_to, up_send, low_recv)
                    add(half, side, z_to, (side, z_to), (low, z_to))

            if step <= 0:

                @pl.when(z < LINE - 1)
                def _():
                    receive(half, high, z_to, down_send, high_recv)
                    add(half, side, z_to, (side, z_to), (high, z_to))

            if step == 0:
                add(half, outs, None, (side, z_to))

        pl.when(inside(step))(work)
        if step > 0:
            send(
                inside(step), half, side, z_to, low, z_to, up_send, low_recv, chip_number(z + 1, y, x)
            )
        if step < 0:
            send(
                inside(step), half, side, z_to, high, z_to, down_send, high_recv, chip_number(z - 1, y, x)
            )

    me = chip_number(z, y, x)
    partners = (
        me * 2 + 1 - core,
        chip_number(z, y, 1 - x) * 2 + core,
        chip_number(z, 1 - y, x) * 2 + core,
    )

    def gain_swap(stage):
        return pltpu.make_async_remote_copy(
            src_ref=gains if stage == 0 else gain_sum.at[stage - 1],
            dst_ref=gain_got.at[stage],
            send_sem=gain_send.at[stage],
            recv_sem=gain_recv.at[stage],
            device_id=(partners[stage],),
            device_id_type=MESH,
        )

    def gain_add(stage):
        gain_swap(stage).wait_recv()
        before = gains[...] if stage == 0 else gain_sum[stage - 1]
        total = before + gain_got[stage]
        if stage < 2:
            gain_sum[stage] = total
            gain_swap(stage + 1).start()
        else:
            gain_line[z] = total

    def gain_pass(slot, sem, z_to):
        return pltpu.make_async_remote_copy(
            src_ref=gain_line.at[slot],
            dst_ref=gain_line.at[slot],
            send_sem=sem.at[slot],
            recv_sem=line_recv.at[slot],
            device_id=(chip_number(z_to, y, x) * 2 + core,),
            device_id_type=MESH,
        )

    def gain_along(step, finish):
        slot = z + step

        def go(copy):
            if finish:
                copy.wait_send()
            else:
                copy.start()

        def work():
            if step != 0 and not finish:
                gain_pass(slot, line_up, z).wait_recv()
            if step >= 0:
                pl.when(z > 0)(lambda: go(gain_pass(slot, line_down, z - 1)))
            if step <= 0:
                pl.when(z < LINE - 1)(lambda: go(gain_pass(slot, line_up, z + 1)))

        pl.when(inside(step))(work)

    gain_swap(0).start()
    for distance in reversed(range(LINE)):
        for step in steps_at(distance):
            for half in range(2):
                y_to, x_to = across(half, 1)
                target = chip_number(z, y_to, x_to)
                z_to = z + step
                first = chip_number(z_to, 1 - y, 1 - x)
                own = chip_number(z_to, y_to, x_to)
                ok = inside(step)
                send(ok, half, ins, first, far, LINE + z_to, far_send, far_recv, target)
                send(ok, half, ins, own, far, z_to, far_send, far_recv, target)
    gain_add(0)
    for distance in (3, 2, 1, 0, -1):
        if distance >= 0:
            for step in steps_at(distance):
                for half in range(2):
                    over_side(half, step)
        if distance < LINE - 1:
            for step in steps_at(distance + 1):
                for half in range(2):
                    over_line(half, step)
        if distance == 3:
            gain_add(1)
        elif distance == 2:
            gain_add(2)
            gain_along(0, False)
        else:
            for step in steps_at(2 - distance):
                gain_along(step, False)
    total = gain_line[0]
    for slot in range(1, LINE):
        total = total + gain_line[slot]
    gains_out[...] = total
    for stage in range(3):
        gain_swap(stage).wait_send()
    for distance in range(LINE):
        for step in steps_at(distance):
            gain_along(step, True)
    for condition, args in pending:

        def finish():
            for copy in copies(*args):
                copy.wait_send()

        pl.when(condition)(finish)


def scatter_chips(blocks, gains):
    dma = pltpu.SemaphoreType.DMA

    def slots(number):
        return [pltpu.VMEM((number,) + item.shape[1:], item.dtype) for item in blocks]

    return pl.pallas_call(
        scatter_kernel,
        out_shape=[jax.ShapeDtypeStruct(item.shape[1:], item.dtype) for item in blocks]
        + [jax.ShapeDtypeStruct(gains.shape, gains.dtype)],
        in_specs=[pl.BlockSpec(memory_space=pltpu.VMEM)] * 4,
        out_specs=[pl.BlockSpec(memory_space=pltpu.VMEM)] * 4,
        scratch_shapes=slots(2 * LINE)
        + slots(LINE)
        + slots(LINE)
        + slots(LINE)
        + [dma((2, 3, 2 * LINE))] * 2
        + [dma((2, 3, LINE))] * 6
        + [
            pltpu.VMEM((2,) + gains.shape, gains.dtype),
            pltpu.VMEM((3,) + gains.shape, gains.dtype),
            pltpu.VMEM((LINE,) + gains.shape, gains.dtype),
            dma((3,)),
            dma((3,)),
            dma((LINE,)),
            dma((LINE,)),
            dma((LINE,)),
        ],
        compiler_params=pltpu.CompilerParams(
            collective_id=2, has_side_effects=True, vmem_limit_bytes=44 * 1024 * 1024
        ),
        name="scatter_chips",
    )(*blocks, gains)


def pad_rows(block, spare):
    return jnp.pad(block, ((0, spare), (0, 0)))


def spread(values, count):
    rows = values.shape[0]
    wide = values.reshape(rows, count, -1)
    return jnp.pad(wide, ((0, 0), (0, 0), (0, BLOCK - wide.shape[2]))).reshape(rows, count * BLOCK)


def gather_in(values, count, width):
    rows = values.shape[0]
    return values.reshape(rows, count, BLOCK)[:, :, :width].reshape(rows, count * width)


def paired_on_device(
    tokens,
    cotangent,
    seq_lengths,
    seq_owner,
    query_weight,
    key_weight,
    value_weight,
    out_weight,
    gate_weight,
    up_weight,
    down_weight,
    attention_gain,
    feedforward_gain,
):
    row_count = tokens.shape[0]
    groups = HEADS // KV_HEADS
    score_scale = 1.0 / math.sqrt(HD)
    count = lax.axis_size("fsdp")
    chips = count // 2
    width = D // count
    units = FF // count
    spare = BLOCK - width
    device = lax.axis_index("fsdp")
    core = device % 2
    swap = [(i, i ^ 1) for i in range(count)]

    def other_core(values):
        return lax.ppermute(values, "fsdp", swap)

    def in_core_order(mine, theirs, axis):
        return jnp.where(
            core == 0,
            jnp.concatenate([mine, theirs], axis=axis),
            jnp.concatenate([theirs, mine], axis=axis),
        )

    def take_core(pair, index):
        return lax.dynamic_index_in_dim(pair, index, axis=0, keepdims=False)

    def row_pair(values):
        split = values.reshape(row_count, chips, 2, BLOCK)
        keep = lax.dynamic_index_in_dim(split, core, axis=2, keepdims=False)
        give = lax.dynamic_index_in_dim(split, 1 - core, axis=2, keepdims=False)
        return jnp.concatenate([keep, other_core(give)], axis=0).reshape(2 * row_count, chips * BLOCK)

    def token_pair(values):
        return jnp.concatenate([values, other_core(values)], axis=0)

    attention_shard = pad_rows(
        jnp.concatenate(
            [
                query_weight.reshape(width, HEADS * HD),
                key_weight.reshape(width, KV_HEADS * HD),
                value_weight.reshape(width, KV_HEADS * HD),
                out_weight.reshape(width, D),
            ],
            axis=1,
        ),
        spare,
    )
    gate_up = jnp.stack([gate_weight.reshape(width, chips, 2, units), up_weight.reshape(width, chips, 2, units)])
    gate_up = gate_up.transpose(3, 0, 1, 2, 4).reshape(2, 2, width, chips * units)
    gate_up = jnp.pad(gate_up, ((0, 0), (0, 0), (0, spare), (0, 0)))
    gate_up_other = other_core(take_core(gate_up, 1 - core))
    gate_up_pair = in_core_order(take_core(gate_up, core), gate_up_other, 1)
    attention_all, gate_up_all, down_all = gather_chips(
        [
            attention_shard,
            gate_up_pair.reshape(4 * BLOCK, chips * units),
            down_weight.reshape(units, D),
        ]
    )
    w_gate = gate_up_all[:, : 2 * BLOCK].reshape(count * BLOCK, chips * units)
    w_up = gate_up_all[:, 2 * BLOCK :].reshape(count * BLOCK, chips * units)
    w_down = down_all.reshape(chips * units, D)

    attention_all = attention_all.reshape(count * BLOCK, 2 * HEADS * HD + 2 * KV_HEADS * HD)
    wide_qkv = (HEADS + 2 * KV_HEADS) * HD
    w_qkv = attention_all[:, :wide_qkv]
    w_out = attention_all[:, wide_qkv:]

    position, row_valid, allowed = own_rows(seq_lengths, seq_owner, device, row_count)
    cosine, sine_table = rope_tables(position, HD)
    grad_out = row_valid[:, None] * cotangent.astype(jnp.float32)
    grad_out_low = grad_out.astype(jnp.bfloat16)
    grad_out_both = jnp.concatenate([grad_out_low, other_core(grad_out_low)], axis=0)

    inputs = tokens.astype(jnp.float32)
    scale_one = rms_scale(inputs)
    normed_one = inputs * scale_one
    low_one = spread((normed_one * attention_gain).astype(jnp.bfloat16), count)
    low_one_pair = row_pair(low_one)
    qkv = jnp.dot(low_one, w_qkv, preferred_element_type=jnp.float32)
    query_pre = qkv[:, : HEADS * HD].reshape(row_count, HEADS, HD)
    key_pre = qkv[:, HEADS * HD : (HEADS + KV_HEADS) * HD].reshape(row_count, KV_HEADS, HD)
    value_low = qkv[:, (HEADS + KV_HEADS) * HD :].astype(jnp.bfloat16).reshape(row_count, KV_HEADS, HD)
    query_low = (
        rotate(query_pre, cosine, sine_table)
        .astype(jnp.bfloat16)
        .reshape(row_count, KV_HEADS, groups, HD)
    )
    key_low = rotate(key_pre, cosine, sine_table).astype(jnp.bfloat16)
    scores = (
        jnp.einsum("ikgd,jkd->kgij", query_low, key_low, preferred_element_type=jnp.float32)
        * score_scale
    )
    masked = jnp.where(allowed[None, None], scores, MASKED_SCORE)
    row_max = jnp.max(masked, axis=-1, keepdims=True)
    exp_scores = jnp.exp(masked - row_max)
    row_total = jnp.sum(exp_scores, axis=-1, keepdims=True)
    probs = exp_scores / row_total
    prob_rows = probs.astype(jnp.bfloat16)
    attended = jnp.einsum(
        "kgij,jkd->ikgd", prob_rows, value_low, preferred_element_type=jnp.float32
    )
    attended_low = spread(attended.reshape(row_count, HEADS * HD).astype(jnp.bfloat16), count)
    attended_pair = row_pair(attended_low)
    middle = inputs + jnp.dot(attended_low, w_out, preferred_element_type=jnp.float32)
    scale_two = rms_scale(middle)
    normed_two = middle * scale_two
    low_two = spread((normed_two * feedforward_gain).astype(jnp.bfloat16), count)
    low_two_both = jnp.concatenate([low_two, other_core(low_two)], axis=0)

    gate_pre = jnp.dot(low_two_both, w_gate, preferred_element_type=jnp.float32)
    upward = jnp.dot(low_two_both, w_up, preferred_element_type=jnp.float32)
    sigmoid_gate = jax.nn.sigmoid(gate_pre)
    silu_gate = gate_pre * sigmoid_gate
    hidden_low = (silu_gate * upward).astype(jnp.bfloat16)
    branch_both = jnp.dot(hidden_low, w_down, preferred_element_type=jnp.float32)
    branch_two = branch_both[:row_count] + other_core(branch_both[row_count:])
    layer_out = (row_valid[:, None] * (middle + branch_two)).astype(jnp.bfloat16)

    grad_wdown = outer_sum(hidden_low, grad_out_both).astype(jnp.bfloat16)
    grad_hidden = times_t(grad_out_both, w_down).astype(jnp.bfloat16).astype(jnp.float32)
    grad_up = (grad_hidden * silu_gate).astype(jnp.bfloat16)
    grad_gate = (
        grad_hidden * upward * sigmoid_gate * (1.0 + gate_pre * (1.0 - sigmoid_gate))
    ).astype(jnp.bfloat16)
    grad_wgate = outer_sum(low_two_both, grad_gate).astype(jnp.bfloat16)
    grad_wup = outer_sum(low_two_both, grad_up).astype(jnp.bfloat16)
    grad_gate_up = jnp.concatenate(
        [
            grad_wgate.reshape(chips, 2 * BLOCK, chips * units),
            grad_wup.reshape(chips, 2 * BLOCK, chips * units),
        ],
        axis=1,
    )
    grad_norm_both = times_t(grad_gate, w_gate) + times_t(grad_up, w_up)
    grad_norm_two = gather_in(
        grad_norm_both[:row_count] + other_core(grad_norm_both[row_count:]), count, width
    )
    grad_gain_two = jnp.sum(grad_norm_two * normed_two, axis=0)
    scaled_two = grad_norm_two * feedforward_gain
    grad_middle = grad_out + scale_two * (
        scaled_two - normed_two * jnp.mean(scaled_two * normed_two, axis=-1, keepdims=True)
    )
    grad_branch_low = grad_middle.astype(jnp.bfloat16)
    grad_wout = outer_sum(attended_pair, token_pair(grad_branch_low)).astype(jnp.bfloat16)
    grad_attended = gather_in(
        times_t(grad_branch_low, w_out).astype(jnp.bfloat16), count, width
    ).reshape(row_count, KV_HEADS, groups, HD)
    grad_value = jnp.einsum(
        "kgij,ikgd->jkd", prob_rows, grad_attended, preferred_element_type=jnp.float32
    )
    grad_probs = jnp.einsum(
        "ikgd,jkd->kgij", grad_attended, value_low, preferred_element_type=jnp.float32
    )
    inner_sum = jnp.sum(probs * grad_probs, axis=-1, keepdims=True)
    grad_scores = (probs * (grad_probs - inner_sum)).astype(jnp.bfloat16)
    grad_query = (
        jnp.einsum("kgij,jkd->ikgd", grad_scores, key_low, preferred_element_type=jnp.float32)
        * score_scale
    )
    grad_key = (
        jnp.einsum("kgij,ikgd->jkd", grad_scores, query_low, preferred_element_type=jnp.float32)
        * score_scale
    )
    grad_qkv = jnp.concatenate(
        [
            unrotate(grad_query.reshape(row_count, HEADS, HD), cosine, sine_table)
            .reshape(row_count, HEADS * HD)
            .astype(jnp.bfloat16),
            unrotate(grad_key, cosine, sine_table)
            .reshape(row_count, KV_HEADS * HD)
            .astype(jnp.bfloat16),
            grad_value.reshape(row_count, KV_HEADS * HD).astype(jnp.bfloat16),
        ],
        axis=1,
    )
    grad_wqkv = outer_sum(low_one_pair, token_pair(grad_qkv)).astype(jnp.bfloat16)
    grad_attention = jnp.concatenate([grad_wqkv, grad_wout], axis=1).reshape(
        chips, BLOCK, 2 * HEADS * HD + 2 * KV_HEADS * HD
    )

    grad_norm_one = gather_in(times_t(grad_qkv, w_qkv), count, width)
    grad_gain_one = jnp.sum(grad_norm_one * normed_one, axis=0)
    scaled_one = grad_norm_one * attention_gain
    grad_inputs = grad_middle + scale_one * (
        scaled_one - normed_one * jnp.mean(scaled_one * normed_one, axis=-1, keepdims=True)
    )
    gain_rows = jnp.concatenate(
        [grad_gain_one[None], grad_gain_two[None], jnp.zeros((6, D), jnp.float32)], axis=0
    )
    attention_sum, gate_up_sum, down_sum, gain_sums = scatter_chips(
        [grad_attention, grad_gate_up, grad_wdown.reshape(chips, units, D)], gain_rows
    )
    attention_sum = attention_sum[:width].astype(jnp.float32)

    gate_up_sum = gate_up_sum.reshape(2, 2, BLOCK, chips * units).transpose(1, 0, 2, 3)
    gate_up_got = other_core(take_core(gate_up_sum, 1 - core))
    gate_up_kept = take_core(gate_up_sum, core)
    halves = in_core_order(gate_up_kept[None], gate_up_got[None], 0)[:, :, :width]
    halves = halves.reshape(2, 2, width, chips, units).transpose(1, 2, 3, 0, 4).astype(jnp.float32)
    edge_key, edge_value = HEADS * HD, (HEADS + KV_HEADS) * HD
    return (
        layer_out,
        grad_inputs.astype(jnp.bfloat16),
        attention_sum[:, :edge_key].reshape(-1),
        attention_sum[:, edge_key:edge_value].reshape(-1),
        attention_sum[:, edge_value:wide_qkv].reshape(-1),
        attention_sum[:, wide_qkv:].reshape(-1),
        halves[0].reshape(-1),
        halves[1].reshape(-1),
        down_sum.astype(jnp.float32).reshape(-1),
        gain_sums[0],
        gain_sums[1],
    )


def solution(mesh):
    count = mesh.shape["fsdp"]
    whole_rows = count == 2 * CHIPS
    program = paired_on_device if whole_rows else on_device
    return jax.shard_map(
        program,
        mesh=mesh,
        in_specs=(
            P("fsdp", None),
            P("fsdp", None),
            P(),
            P(),
            P("fsdp"),
            P("fsdp"),
            P("fsdp"),
            P("fsdp"),
            P("fsdp"),
            P("fsdp"),
            P("fsdp"),
            P(),
            P(),
        ),
        out_specs=(
            P("fsdp", None),
            P("fsdp", None),
            P("fsdp"),
            P("fsdp"),
            P("fsdp"),
            P("fsdp"),
            P("fsdp"),
            P("fsdp"),
            P("fsdp"),
            P(),
            P(),
        ),
        check_vma=False,
    )
```

```python
import math

import jax
import jax.numpy as jnp
from jax import lax
from jax.experimental import pallas as pl
from jax.experimental.pallas import tpu as pltpu
from jax.sharding import PartitionSpec as P

D = 960
HEADS = 15
KV_HEADS = 5
HD = 64
FF = 2560


EPSILON = 1e-05
ROPE_BASE = 10000.0
MASKED_SCORE = -1e30


def own_rows(seq_lengths, seq_owner, device, row_count):
    seq_count = seq_lengths.shape[0]
    seq_index = jnp.arange(seq_count, dtype=jnp.int32)
    is_mine = seq_owner == device
    first_seq = jnp.min(jnp.where(is_mine, seq_index, seq_count))
    second_seq = jnp.min(jnp.where(is_mine & (seq_index != first_seq), seq_index, seq_count))
    len_first = jnp.sum(jnp.where(seq_index == first_seq, seq_lengths, 0))
    len_second = jnp.sum(jnp.where(seq_index == second_seq, seq_lengths, 0))
    row_index = jnp.arange(row_count, dtype=jnp.int32)
    segment = (row_index >= len_first).astype(jnp.int32) + (
        row_index >= len_first + len_second
    ).astype(jnp.int32)
    seg_start = jnp.where(
        segment == 0, 0, jnp.where(segment == 1, len_first, len_first + len_second)
    )
    position = row_index - seg_start
    row_valid = (segment < 2).astype(jnp.float32)
    allowed = (segment[:, None] == segment[None, :]) & (row_index[None, :] <= row_index[:, None])
    return (position, row_valid, allowed)


def rope_tables(position, head_size):
    half_size = head_size // 2
    frequency = ROPE_BASE ** (-jnp.arange(half_size, dtype=jnp.float32) * 2.0 / head_size)
    angles = position.astype(jnp.float32)[:, None] * frequency[None, :]
    return (jnp.cos(angles), jnp.sin(angles))


def rotate(values, cosine, sine_table):
    half_size = values.shape[-1] // 2
    front_half = values[..., :half_size]
    back_half = values[..., half_size:]
    cos_part = cosine[:, None, :]
    sin_part = sine_table[:, None, :]
    return jnp.concatenate(
        [
            front_half * cos_part - back_half * sin_part,
            back_half * cos_part + front_half * sin_part,
        ],
        axis=-1,
    )


def unrotate(gradient, cosine, sine_table):
    half_size = gradient.shape[-1] // 2
    front_half = gradient[..., :half_size]
    back_half = gradient[..., half_size:]
    cos_part = cosine[:, None, :]
    sin_part = sine_table[:, None, :]
    return jnp.concatenate(
        [
            front_half * cos_part + back_half * sin_part,
            back_half * cos_part - front_half * sin_part,
        ],
        axis=-1,
    )


def rms_scale(values):
    return lax.rsqrt(jnp.mean(values * values, axis=-1, keepdims=True) + EPSILON)


def outer_sum(left_side, right_side):
    return lax.dot_general(
        left_side, right_side, (((0,), (0,)), ((), ())), preferred_element_type=jnp.float32
    )


def times_t(left_side, right_side):
    return lax.dot_general(
        left_side, right_side, (((1,), (1,)), ((), ())), preferred_element_type=jnp.float32
    )


def pack_shards(shard_list):
    return jnp.concatenate([piece.reshape(1, -1) for piece in shard_list], axis=1)


def unpack_gathered(whole, shard_list):
    result_list = []
    offset = 0
    for piece in shard_list:
        width = piece.shape[0]
        result_list.append(whole[:, offset : offset + width].reshape(-1))
        offset = offset + width
    return result_list


def pack_grads(grad_list, count):
    return jnp.concatenate([item.reshape(count, -1) for item in grad_list], axis=1)


def unpack_grads(summed, grad_list, count):
    result_list = []
    offset = 0
    for item in grad_list:
        width = item.size // count
        result_list.append(summed[:, offset : offset + width].reshape(-1))
        offset = offset + width
    return result_list


def shape_weights(flat_list):
    query_flat, key_flat, value_flat, out_flat, gate_flat, up_flat, down_flat = flat_list
    return (
        query_flat.reshape(D, HEADS * HD),
        key_flat.reshape(D, KV_HEADS * HD),
        value_flat.reshape(D, KV_HEADS * HD),
        out_flat.reshape(HEADS * HD, D),
        gate_flat.reshape(D, FF),
        up_flat.reshape(D, FF),
        down_flat.reshape(FF, D),
    )


def on_device(
    tokens,
    cotangent,
    seq_lengths,
    seq_owner,
    query_weight,
    key_weight,
    value_weight,
    out_weight,
    gate_weight,
    up_weight,
    down_weight,
    attention_gain,
    feedforward_gain,
):
    row_count = tokens.shape[0]
    groups = HEADS // KV_HEADS
    score_scale = 1.0 / math.sqrt(HD)
    count = lax.axis_size("fsdp")
    device = lax.axis_index("fsdp")
    position, row_valid, allowed = own_rows(seq_lengths, seq_owner, device, row_count)
    cosine, sine_table = rope_tables(position, HD)
    shard_list = (
        query_weight,
        key_weight,
        value_weight,
        out_weight,
        gate_weight,
        up_weight,
        down_weight,
    )
    gathered = lax.all_gather(pack_shards(shard_list), "fsdp", axis=0, tiled=True)
    w_query, w_key, w_value, w_out, w_gate, w_up, w_down = shape_weights(
        unpack_gathered(gathered, shard_list)
    )
    inputs = tokens.astype(jnp.float32)
    scale_one = rms_scale(inputs)
    normed_one = inputs * scale_one
    low_one = (normed_one * attention_gain).astype(jnp.bfloat16)
    query_pre = jnp.dot(low_one, w_query, preferred_element_type=jnp.float32).reshape(
        row_count, HEADS, HD
    )
    key_pre = jnp.dot(low_one, w_key, preferred_element_type=jnp.float32).reshape(
        row_count, KV_HEADS, HD
    )
    value_low = (
        jnp.dot(low_one, w_value, preferred_element_type=jnp.float32)
        .astype(jnp.bfloat16)
        .reshape(row_count, KV_HEADS, HD)
    )
    query_low = (
        rotate(query_pre, cosine, sine_table)
        .astype(jnp.bfloat16)
        .reshape(row_count, KV_HEADS, groups, HD)
    )
    key_low = rotate(key_pre, cosine, sine_table).astype(jnp.bfloat16)
    scores = (
        jnp.einsum("ikgd,jkd->kgij", query_low, key_low, preferred_element_type=jnp.float32)
        * score_scale
    )
    masked = jnp.where(allowed[None, None], scores, MASKED_SCORE)
    row_max = jnp.max(masked, axis=-1, keepdims=True)
    exp_scores = jnp.exp(masked - row_max)
    row_total = jnp.sum(exp_scores, axis=-1, keepdims=True)
    log_total = row_max + jnp.log(row_total)
    prob_rows = (exp_scores / row_total).astype(jnp.bfloat16)
    attended = jnp.einsum(
        "kgij,jkd->ikgd", prob_rows, value_low, preferred_element_type=jnp.float32
    )
    attended_low = attended.reshape(row_count, HEADS * HD).astype(jnp.bfloat16)
    middle = inputs + jnp.dot(attended_low, w_out, preferred_element_type=jnp.float32)
    scale_two = rms_scale(middle)
    normed_two = middle * scale_two
    low_two = (normed_two * feedforward_gain).astype(jnp.bfloat16)
    gate_pre = jnp.dot(low_two, w_gate, preferred_element_type=jnp.float32)
    upward = jnp.dot(low_two, w_up, preferred_element_type=jnp.float32)
    sigmoid_gate = jax.nn.sigmoid(gate_pre)
    silu_gate = gate_pre * sigmoid_gate
    hidden_low = (silu_gate * upward).astype(jnp.bfloat16)
    branch_two = jnp.dot(hidden_low, w_down, preferred_element_type=jnp.float32)
    layer_out = (row_valid[:, None] * (middle + branch_two)).astype(jnp.bfloat16)
    grad_out = row_valid[:, None] * cotangent.astype(jnp.float32)
    grad_out_low = grad_out.astype(jnp.bfloat16)
    grad_wdown = outer_sum(hidden_low, grad_out_low)
    grad_hidden = times_t(grad_out_low, w_down).astype(jnp.bfloat16).astype(jnp.float32)
    grad_up = (grad_hidden * silu_gate).astype(jnp.bfloat16)
    grad_gate = (
        grad_hidden * upward * sigmoid_gate * (1.0 + gate_pre * (1.0 - sigmoid_gate))
    ).astype(jnp.bfloat16)
    grad_wgate = outer_sum(low_two, grad_gate)
    grad_wup = outer_sum(low_two, grad_up)
    grad_norm_two = times_t(grad_gate, w_gate) + times_t(grad_up, w_up)
    grad_gain_two = jnp.sum(grad_norm_two * normed_two, axis=0)
    scaled_two = grad_norm_two * feedforward_gain
    grad_middle = grad_out + scale_two * (
        scaled_two - normed_two * jnp.mean(scaled_two * normed_two, axis=-1, keepdims=True)
    )
    grad_branch_low = grad_middle.astype(jnp.bfloat16)
    grad_wout = outer_sum(attended_low, grad_branch_low)
    grad_attended = (
        times_t(grad_branch_low, w_out)
        .astype(jnp.bfloat16)
        .reshape(row_count, KV_HEADS, groups, HD)
    )
    scores_again = (
        jnp.einsum("ikgd,jkd->kgij", query_low, key_low, preferred_element_type=jnp.float32)
        * score_scale
    )
    probs_again = jnp.exp(jnp.where(allowed[None, None], scores_again, MASKED_SCORE) - log_total)
    grad_value = jnp.einsum(
        "kgij,ikgd->jkd",
        probs_again.astype(jnp.bfloat16),
        grad_attended,
        preferred_element_type=jnp.float32,
    )
    grad_probs = jnp.einsum(
        "ikgd,jkd->kgij", grad_attended, value_low, preferred_element_type=jnp.float32
    )
    inner_sum = jnp.sum(probs_again * grad_probs, axis=-1, keepdims=True)
    grad_scores = (probs_again * (grad_probs - inner_sum)).astype(jnp.bfloat16)
    grad_query = (
        jnp.einsum("kgij,jkd->ikgd", grad_scores, key_low, preferred_element_type=jnp.float32)
        * score_scale
    )
    grad_key = (
        jnp.einsum("kgij,ikgd->jkd", grad_scores, query_low, preferred_element_type=jnp.float32)
        * score_scale
    )
    grad_query_low = (
        unrotate(grad_query.reshape(row_count, HEADS, HD), cosine, sine_table)
        .reshape(row_count, HEADS * HD)
        .astype(jnp.bfloat16)
    )
    grad_key_low = (
        unrotate(grad_key, cosine, sine_table)
        .reshape(row_count, KV_HEADS * HD)
        .astype(jnp.bfloat16)
    )
    grad_value_low = grad_value.reshape(row_count, KV_HEADS * HD).astype(jnp.bfloat16)
    grad_wquery = outer_sum(low_one, grad_query_low)
    grad_wkey = outer_sum(low_one, grad_key_low)
    grad_wvalue = outer_sum(low_one, grad_value_low)
    grad_norm_one = (
        times_t(grad_query_low, w_query)
        + times_t(grad_key_low, w_key)
        + times_t(grad_value_low, w_value)
    )
    grad_gain_one = jnp.sum(grad_norm_one * normed_one, axis=0)
    scaled_one = grad_norm_one * attention_gain
    grad_inputs = grad_middle + scale_one * (
        scaled_one - normed_one * jnp.mean(scaled_one * normed_one, axis=-1, keepdims=True)
    )
    gain_one_sum, gain_two_sum = lax.psum((grad_gain_one, grad_gain_two), "fsdp")
    every_list = (grad_wquery, grad_wkey, grad_wvalue, grad_wout, grad_wgate, grad_wup, grad_wdown)
    every_summed = lax.psum_scatter(
        pack_grads(every_list, count), "fsdp", scatter_dimension=0, tiled=True
    )
    query_shard, key_shard, value_shard, out_shard, gate_shard, up_shard, down_shard = unpack_grads(
        every_summed, every_list, count
    )
    return (
        layer_out,
        grad_inputs.astype(jnp.bfloat16),
        query_shard,
        key_shard,
        value_shard,
        out_shard,
        gate_shard,
        up_shard,
        down_shard,
        gain_one_sum,
        gain_two_sum,
    )


BLOCK = 32
LINE = 4
CHIPS = 16
MESH = pl.DeviceIdType.MESH


def chip_place():
    device = lax.axis_index("fsdp")
    core, chip = device % 2, device // 2
    return core, chip // 4, (chip // 2) % 2, chip % 2


def chip_number(z, y, x):
    return (z * 2 + y) * 2 + x


def greet_neighbours(core, z, y, x):
    barrier = pltpu.get_barrier_semaphore()

    def greet(z_to, y_to, x_to, core_to=core):
        pl.semaphore_signal(
            barrier,
            inc=1,
            device_id=(chip_number(z_to, y_to, x_to) * 2 + core_to,),
            device_id_type=MESH,
        )

    greet(z, y, x, 1 - core)
    greet(z, 1 - y, x)
    greet(z, y, 1 - x)

    @pl.when(z > 0)
    def _():
        greet(z - 1, y, x)

    @pl.when(z < LINE - 1)
    def _():
        greet(z + 1, y, x)

    pl.semaphore_wait(barrier, jnp.where((z > 0) & (z < LINE - 1), 5, 4))


def half_rows(refs, half):
    result = []
    for ref in refs:
        rows = ref.shape[-2]
        first = (rows // 2 + 15) // 16 * 16
        result.append(pl.ds(0, first) if half == 0 else pl.ds(first, rows - first))
    return result


def steps_at(distance):
    return (0,) if distance == 0 else (-distance, distance)


def gather_kernel(*refs):
    ins, outs = refs[0:3], refs[3:6]
    own_sem, recv_sem, up_sem, down_sem, first_sem, second_sem, pair_send, pair_recv = refs[6:]
    core, z, y, x = chip_place()
    greet_neighbours(core, z, y, x)
    me = chip_number(z, y, x)
    rows = [half_rows(ins, half) for half in range(2)]
    pending = []

    def out_at(i, source, span, side=core):
        return outs[0].at[source, side, span] if i == 0 else outs[i].at[source, span]

    def to_pair(half, source, is_own):
        span = rows[half][0]
        return pltpu.make_async_remote_copy(
            src_ref=ins[0].at[span] if is_own else out_at(0, source, span),
            dst_ref=out_at(0, source, span),
            send_sem=pair_send.at[half, source],
            recv_sem=pair_recv.at[half, source],
            device_id=(me * 2 + 1 - core,),
            device_id_type=MESH,
        )

    def send(half, source, is_own, sem, slot, target):
        for i in range(3):
            span = rows[half][i]
            src = ins[i].at[span] if is_own else out_at(i, source, span)
            copy = pltpu.make_async_remote_copy(
                src_ref=src,
                dst_ref=out_at(i, source, span),
                send_sem=sem.at[half, i, slot],
                recv_sem=recv_sem.at[half, i, source],
                device_id=(target * 2 + core,),
                device_id_type=MESH,
            )
            copy.start()
            yield copy

    def send_all(condition, *args):
        def run():
            for _ in send(*args):
                pass

        if condition is None:
            run()
        else:
            pl.when(condition)(run)
        pending.append((condition, args))

    def receive(half, source):
        for i in range(3):
            view = out_at(i, source, rows[half][i])
            pltpu.make_async_remote_copy(
                src_ref=view,
                dst_ref=view,
                send_sem=own_sem.at[i],
                recv_sem=recv_sem.at[half, i, source],
                device_id=(me * 2 + 1 - core,),
                device_id_type=MESH,
            ).wait_recv()
        to_pair(half, source, False).start()

    def across(half, place):
        return (1 - y, x) if (half == 0) == (place == 0) else (y, 1 - x)

    def inside(step):
        return (z + step >= 0) & (z + step < LINE)

    def spread_line(half, step):
        z_from = z + step
        source = chip_number(z_from, y, x)
        own = step == 0
        ok = None if own else inside(step)
        if step >= 0:
            cond = z > 0 if own else (ok & (z > 0))
            send_all(cond, half, source, own, down_sem, z_from, chip_number(z - 1, y, x))
        if step <= 0:
            cond = z < LINE - 1 if own else (ok & (z < LINE - 1))
            send_all(cond, half, source, own, up_sem, z_from, chip_number(z + 1, y, x))
        send_all(ok, half, source, own, first_sem, z_from, chip_number(z, *across(half, 0)))
        send_all(ok, half, source, own, second_sem, z_from, chip_number(z, *across(half, 1)))

    def spread_side(half, step):
        z_from = z + step
        source = chip_number(z_from, *across(half, 0))
        ok = None if step == 0 else inside(step)
        if ok is None:
            receive(half, source)
        else:
            pl.when(ok)(lambda: receive(half, source))
        send_all(
            ok, half, source, False, second_sem, LINE + z_from, chip_number(z, *across(half, 1))
        )

    whole = [pl.ds(0, ref.shape[0]) for ref in ins]
    local = [
        pltpu.make_async_copy(ins[i], out_at(i, me, whole[i]), own_sem.at[i]) for i in range(3)
    ]
    for half in range(2):
        spread_line(half, 0)
        to_pair(half, me, True).start()
    for copy in local:
        copy.start()
    for distance in range(LINE):
        if distance > 0:
            for half in range(2):
                for step in steps_at(distance):
                    pl.when(inside(step))(
                        lambda: receive(half, chip_number(z + step, y, x))
                    )
                    spread_line(half, step)
        for half in range(2):
            for step in steps_at(distance):
                spread_side(half, step)
    for half in range(2):
        y_far, x_far = across(half, 1)
        for z_from in range(LINE):
            receive(half, chip_number(z_from, y_far, x_far))
            receive(half, chip_number(z_from, 1 - y, 1 - x))
    for copy in local:
        copy.wait()
    for half in range(2):
        span = rows[half][0]
        for source in range(CHIPS):
            view = out_at(0, source, span, 1 - core)
            pltpu.make_async_remote_copy(
                src_ref=view,
                dst_ref=view,
                send_sem=pair_send.at[half, source],
                recv_sem=pair_recv.at[half, source],
                device_id=(me * 2 + 1 - core,),
                device_id_type=MESH,
            ).wait_recv()
            to_pair(half, source, False).wait_send()
    for condition, (half, source, is_own, sem, slot, target) in pending:

        def finish():
            for i in range(3):
                span = rows[half][i]
                src = ins[i].at[span] if is_own else out_at(i, source, span)
                pltpu.make_async_remote_copy(
                    src_ref=src,
                    dst_ref=out_at(i, source, span),
                    send_sem=sem.at[half, i, slot],
                    recv_sem=recv_sem.at[half, i, source],
                    device_id=(target * 2 + core,),
                    device_id_type=MESH,
                ).wait_send()

        if condition is None:
            finish()
        else:
            pl.when(condition)(finish)


def gather_chips(blocks):
    dma = pltpu.SemaphoreType.DMA
    return pl.pallas_call(
        gather_kernel,
        out_shape=[
            jax.ShapeDtypeStruct((CHIPS,) + extra + item.shape, item.dtype)
            for item, extra in zip(blocks, ((2,), (), ()))
        ],
        in_specs=[pl.BlockSpec(memory_space=pl.ANY)] * 3,
        out_specs=[pl.BlockSpec(memory_space=pl.ANY)] * 3,
        scratch_shapes=[
            dma((3,)),
            dma((2, 3, CHIPS)),
            dma((2, 3, LINE)),
            dma((2, 3, LINE)),
            dma((2, 3, LINE)),
            dma((2, 3, 2 * LINE)),
            dma((2, CHIPS)),
            dma((2, CHIPS)),
        ],
        compiler_params=pltpu.CompilerParams(collective_id=1, has_side_effects=True),
        name="gather_chips",
    )(*blocks)


def scatter_kernel(*refs):
    ins, gains, outs, gains_out = refs[0:3], refs[3], refs[4:7], refs[7]
    far, side, low, high = refs[8:11], refs[11:14], refs[14:17], refs[17:20]
    far_send, far_recv, side_send, side_recv, up_send, low_recv, down_send, high_recv = refs[20:28]
    gain_sum, gain_got, gain_line, gain_send, gain_recv, line_up, line_down, line_recv = refs[28:]
    core, z, y, x = chip_place()
    greet_neighbours(core, z, y, x)
    rows = [half_rows(outs, half) for half in range(2)]
    pending = []

    def across(half, place):
        return (1 - y, x) if (half == 0) == (place == 0) else (y, 1 - x)

    def inside(step):
        return (z + step >= 0) & (z + step < LINE)

    def copies(half, source, source_at, buffer, slot, send_sem, recv_sem, target):
        return [
            pltpu.make_async_remote_copy(
                src_ref=source[i].at[source_at, rows[half][i]],
                dst_ref=buffer[i].at[slot, rows[half][i]],
                send_sem=send_sem.at[half, i, slot],
                recv_sem=recv_sem.at[half, i, slot],
                device_id=(target * 2 + core,),
                device_id_type=MESH,
            )
            for i in range(3)
        ]

    def send(condition, *args):
        def run():
            for copy in copies(*args):
                copy.start()

        pl.when(condition)(run)
        pending.append((condition, args))

    def receive(half, buffer, slot, send_sem, recv_sem):
        for copy in copies(half, buffer, slot, buffer, slot, send_sem, recv_sem, 0):
            copy.wait_recv()

    def add(half, result, result_at, *terms):
        for i in range(3):
            span = rows[half][i]
            total = None
            for buffer, slot in terms:
                value = buffer[i][slot, span, :].astype(jnp.float32)
                total = value if total is None else total + value
            if result_at is None:
                result[i][span, :] = total.astype(jnp.bfloat16)
            else:
                result[i][result_at, span, :] = total.astype(jnp.bfloat16)

    def over_side(half, step):
        z_to = z + step
        place = across(half, 0)

        def work():
            receive(half, far, LINE + z_to, far_send, far_recv)
            add(half, far, LINE + z_to, (far, LINE + z_to), (ins, chip_number(z_to, *place)))

        pl.when(inside(step))(work)
        send(
            inside(step), half, far, LINE + z_to, side, z_to, side_send, side_recv, chip_number(z, *place)
        )

    def over_line(half, step):
        z_to = z + step

        def work():
            receive(half, far, z_to, far_send, far_recv)
            receive(half, side, z_to, side_send, side_recv)
            add(
                half, side, z_to, (side, z_to), (far, z_to), (ins, chip_number(z_to, y, x))
            )
            if step >= 0:

                @pl.when(z > 0)
                def _():
                    receive(half, low, z_to, up_send, low_recv)
                    add(half, side, z_to, (side, z_to), (low, z_to))

            if step <= 0:

                @pl.when(z < LINE - 1)
                def _():
                    receive(half, high, z_to, down_send, high_recv)
                    add(half, side, z_to, (side, z_to), (high, z_to))

            if step == 0:
                add(half, outs, None, (side, z_to))

        pl.when(inside(step))(work)
        if step > 0:
            send(
                inside(step), half, side, z_to, low, z_to, up_send, low_recv, chip_number(z + 1, y, x)
            )
        if step < 0:
            send(
                inside(step), half, side, z_to, high, z_to, down_send, high_recv, chip_number(z - 1, y, x)
            )

    me = chip_number(z, y, x)
    partners = (
        me * 2 + 1 - core,
        chip_number(z, y, 1 - x) * 2 + core,
        chip_number(z, 1 - y, x) * 2 + core,
    )

    def gain_swap(stage):
        return pltpu.make_async_remote_copy(
            src_ref=gains if stage == 0 else gain_sum.at[stage - 1],
            dst_ref=gain_got.at[stage],
            send_sem=gain_send.at[stage],
            recv_sem=gain_recv.at[stage],
            device_id=(partners[stage],),
            device_id_type=MESH,
        )

    def gain_add(stage):
        gain_swap(stage).wait_recv()
        before = gains[...] if stage == 0 else gain_sum[stage - 1]
        total = before + gain_got[stage]
        if stage < 2:
            gain_sum[stage] = total
            gain_swap(stage + 1).start()
        else:
            gain_line[z] = total

    def gain_pass(slot, sem, z_to):
        return pltpu.make_async_remote_copy(
            src_ref=gain_line.at[slot],
            dst_ref=gain_line.at[slot],
            send_sem=sem.at[slot],
            recv_sem=line_recv.at[slot],
            device_id=(chip_number(z_to, y, x) * 2 + core,),
            device_id_type=MESH,
        )

    def gain_along(step, finish):
        slot = z + step

        def go(copy):
            if finish:
                copy.wait_send()
            else:
                copy.start()

        def work():
            if step != 0 and not finish:
                gain_pass(slot, line_up, z).wait_recv()
            if step >= 0:
                pl.when(z > 0)(lambda: go(gain_pass(slot, line_down, z - 1)))
            if step <= 0:
                pl.when(z < LINE - 1)(lambda: go(gain_pass(slot, line_up, z + 1)))

        pl.when(inside(step))(work)

    gain_swap(0).start()
    for distance in reversed(range(LINE)):
        for step in steps_at(distance):
            for half in range(2):
                y_to, x_to = across(half, 1)
                target = chip_number(z, y_to, x_to)
                z_to = z + step
                first = chip_number(z_to, 1 - y, 1 - x)
                ok = inside(step)
                send(ok, half, ins, first, far, LINE + z_to, far_send, far_recv, target)
    gain_add(0)
    for distance in (3, 2, 1, 0, -1):
        if distance >= 0:
            for step in steps_at(distance):
                for half in range(2):
                    over_side(half, step)
            for step in steps_at(distance):
                for half in range(2):
                    target = chip_number(z, *across(half, 1))
                    own = chip_number(z + step, *across(half, 1))
                    send(
                        inside(step), half, ins, own, far, z + step, far_send, far_recv, target
                    )
        if distance < LINE - 1:
            for step in steps_at(distance + 1):
                for half in range(2):
                    over_line(half, step)
        if distance == 3:
            gain_add(1)
        elif distance == 2:
            gain_add(2)
            gain_along(0, False)
        else:
            for step in steps_at(2 - distance):
                gain_along(step, False)
    total = gain_line[0]
    for slot in range(1, LINE):
        total = total + gain_line[slot]
    gains_out[...] = total
    for stage in range(3):
        gain_swap(stage).wait_send()
    for distance in range(LINE):
        for step in steps_at(distance):
            gain_along(step, True)
    for condition, args in pending:

        def finish():
            for copy in copies(*args):
                copy.wait_send()

        pl.when(condition)(finish)


def scatter_chips(blocks, gains):
    dma = pltpu.SemaphoreType.DMA

    def slots(number):
        return [pltpu.VMEM((number,) + item.shape[1:], item.dtype) for item in blocks]

    return pl.pallas_call(
        scatter_kernel,
        out_shape=[jax.ShapeDtypeStruct(item.shape[1:], item.dtype) for item in blocks]
        + [jax.ShapeDtypeStruct(gains.shape, gains.dtype)],
        in_specs=[pl.BlockSpec(memory_space=pltpu.VMEM)] * 4,
        out_specs=[pl.BlockSpec(memory_space=pltpu.VMEM)] * 4,
        scratch_shapes=slots(2 * LINE)
        + slots(LINE)
        + slots(LINE)
        + slots(LINE)
        + [dma((2, 3, 2 * LINE))] * 2
        + [dma((2, 3, LINE))] * 6
        + [
            pltpu.VMEM((2,) + gains.shape, gains.dtype),
            pltpu.VMEM((3,) + gains.shape, gains.dtype),
            pltpu.VMEM((LINE,) + gains.shape, gains.dtype),
            dma((3,)),
            dma((3,)),
            dma((LINE,)),
            dma((LINE,)),
            dma((LINE,)),
        ],
        compiler_params=pltpu.CompilerParams(
            collective_id=2, has_side_effects=True, vmem_limit_bytes=44 * 1024 * 1024
        ),
        name="scatter_chips",
    )(*blocks, gains)


def pad_rows(block, spare):
    return jnp.pad(block, ((0, spare), (0, 0)))


def spread(values, count):
    rows = values.shape[0]
    wide = values.reshape(rows, count, -1)
    return jnp.pad(wide, ((0, 0), (0, 0), (0, BLOCK - wide.shape[2]))).reshape(rows, count * BLOCK)


def gather_in(values, count, width):
    rows = values.shape[0]
    return values.reshape(rows, count, BLOCK)[:, :, :width].reshape(rows, count * width)


def paired_on_device(
    tokens,
    cotangent,
    seq_lengths,
    seq_owner,
    query_weight,
    key_weight,
    value_weight,
    out_weight,
    gate_weight,
    up_weight,
    down_weight,
    attention_gain,
    feedforward_gain,
):
    row_count = tokens.shape[0]
    groups = HEADS // KV_HEADS
    score_scale = 1.0 / math.sqrt(HD)
    count = lax.axis_size("fsdp")
    chips = count // 2
    width = D // count
    units = FF // count
    spare = BLOCK - width
    device = lax.axis_index("fsdp")
    core = device % 2
    swap = [(i, i ^ 1) for i in range(count)]

    def other_core(values):
        return lax.ppermute(values, "fsdp", swap)

    def in_core_order(mine, theirs, axis):
        return jnp.where(
            core == 0,
            jnp.concatenate([mine, theirs], axis=axis),
            jnp.concatenate([theirs, mine], axis=axis),
        )

    def take_core(pair, index):
        return lax.dynamic_index_in_dim(pair, index, axis=0, keepdims=False)

    def row_pair(values):
        split = values.reshape(row_count, chips, 2, BLOCK)
        keep = lax.dynamic_index_in_dim(split, core, axis=2, keepdims=False)
        give = lax.dynamic_index_in_dim(split, 1 - core, axis=2, keepdims=False)
        return jnp.concatenate([keep, other_core(give)], axis=0).reshape(2 * row_count, chips * BLOCK)

    def token_pair(values):
        return jnp.concatenate([values, other_core(values)], axis=0)

    attention_shard = pad_rows(
        jnp.concatenate(
            [
                query_weight.reshape(width, HEADS * HD),
                key_weight.reshape(width, KV_HEADS * HD),
                value_weight.reshape(width, KV_HEADS * HD),
                out_weight.reshape(width, D),
            ],
            axis=1,
        ),
        spare,
    )
    gate_up = jnp.concatenate(
        [
            item.reshape(width, chips, 2, units).transpose(2, 0, 1, 3).reshape(2, width, chips * units)
            for item in (gate_weight, up_weight)
        ],
        axis=2,
    )
    gate_up = jnp.pad(gate_up, ((0, 0), (0, spare), (0, 0)))
    gate_up_other = other_core(take_core(gate_up, 1 - core))
    gate_up_pair = in_core_order(take_core(gate_up, core), gate_up_other, 0)
    attention_all, gate_up_all, down_all = gather_chips(
        [
            attention_shard,
            gate_up_pair,
            down_weight.reshape(units, D),
        ]
    )
    w_gate_up = gate_up_all.reshape(count * BLOCK, 2 * chips * units)
    w_down = down_all.reshape(chips * units, D)

    attention_all = attention_all.reshape(count * BLOCK, 2 * HEADS * HD + 2 * KV_HEADS * HD)
    wide_qkv = (HEADS + 2 * KV_HEADS) * HD
    w_qkv = attention_all[:, :wide_qkv]
    w_out = attention_all[:, wide_qkv:]

    position, row_valid, allowed = own_rows(seq_lengths, seq_owner, device, row_count)
    cosine, sine_table = rope_tables(position, HD)
    grad_out = row_valid[:, None] * cotangent.astype(jnp.float32)
    grad_out_low = grad_out.astype(jnp.bfloat16)
    grad_out_both = jnp.concatenate([grad_out_low, other_core(grad_out_low)], axis=0)

    inputs = tokens.astype(jnp.float32)
    scale_one = rms_scale(inputs)
    normed_one = inputs * scale_one
    low_one = spread((normed_one * attention_gain).astype(jnp.bfloat16), count)
    low_one_pair = row_pair(low_one)
    qkv = jnp.dot(low_one, w_qkv, preferred_element_type=jnp.float32)
    query_pre = qkv[:, : HEADS * HD].reshape(row_count, HEADS, HD)
    key_pre = qkv[:, HEADS * HD : (HEADS + KV_HEADS) * HD].reshape(row_count, KV_HEADS, HD)
    value_low = qkv[:, (HEADS + KV_HEADS) * HD :].astype(jnp.bfloat16).reshape(row_count, KV_HEADS, HD)
    query_low = (
        rotate(query_pre, cosine, sine_table)
        .astype(jnp.bfloat16)
        .reshape(row_count, KV_HEADS, groups, HD)
    )
    key_low = rotate(key_pre, cosine, sine_table).astype(jnp.bfloat16)
    scores = (
        jnp.einsum("ikgd,jkd->kgij", query_low, key_low, preferred_element_type=jnp.float32)
        * score_scale
    )
    masked = jnp.where(allowed[None, None], scores, MASKED_SCORE)
    row_max = jnp.max(masked, axis=-1, keepdims=True)
    exp_scores = jnp.exp(masked - row_max)
    row_total = jnp.sum(exp_scores, axis=-1, keepdims=True)
    probs = exp_scores / row_total
    prob_rows = probs.astype(jnp.bfloat16)
    attended = jnp.einsum(
        "kgij,jkd->ikgd", prob_rows, value_low, preferred_element_type=jnp.float32
    )
    attended_low = spread(attended.reshape(row_count, HEADS * HD).astype(jnp.bfloat16), count)
    attended_pair = row_pair(attended_low)
    middle = inputs + jnp.dot(attended_low, w_out, preferred_element_type=jnp.float32)
    scale_two = rms_scale(middle)
    normed_two = middle * scale_two
    low_two = spread((normed_two * feedforward_gain).astype(jnp.bfloat16), count)
    low_two_both = jnp.concatenate([low_two, other_core(low_two)], axis=0)

    gate_and_up = jnp.dot(low_two_both, w_gate_up, preferred_element_type=jnp.float32)
    gate_pre = gate_and_up[:, : chips * units]
    upward = gate_and_up[:, chips * units :]
    sigmoid_gate = jax.nn.sigmoid(gate_pre)
    silu_gate = gate_pre * sigmoid_gate
    hidden_low = (silu_gate * upward).astype(jnp.bfloat16)
    branch_both = jnp.dot(hidden_low, w_down, preferred_element_type=jnp.float32)
    branch_two = branch_both[:row_count] + other_core(branch_both[row_count:])
    layer_out = (row_valid[:, None] * (middle + branch_two)).astype(jnp.bfloat16)

    grad_wdown = outer_sum(hidden_low, grad_out_both).astype(jnp.bfloat16)
    grad_hidden = times_t(grad_out_both, w_down).astype(jnp.bfloat16).astype(jnp.float32)
    grad_up = (grad_hidden * silu_gate).astype(jnp.bfloat16)
    grad_gate = (
        grad_hidden * upward * sigmoid_gate * (1.0 + gate_pre * (1.0 - sigmoid_gate))
    ).astype(jnp.bfloat16)
    grad_both = jnp.concatenate([grad_gate, grad_up], axis=1)
    grad_gate_up = (
        outer_sum(low_two_both, grad_both)
        .astype(jnp.bfloat16)
        .reshape(chips, 2 * BLOCK, 2 * chips * units)
    )
    grad_norm_both = times_t(grad_both, w_gate_up)
    grad_norm_two = gather_in(
        grad_norm_both[:row_count] + other_core(grad_norm_both[row_count:]), count, width
    )
    grad_gain_two = jnp.sum(grad_norm_two * normed_two, axis=0)
    scaled_two = grad_norm_two * feedforward_gain
    grad_middle = grad_out + scale_two * (
        scaled_two - normed_two * jnp.mean(scaled_two * normed_two, axis=-1, keepdims=True)
    )
    grad_branch_low = grad_middle.astype(jnp.bfloat16)
    grad_wout = outer_sum(attended_pair, token_pair(grad_branch_low)).astype(jnp.bfloat16)
    grad_attended = gather_in(
        times_t(grad_branch_low, w_out).astype(jnp.bfloat16), count, width
    ).reshape(row_count, KV_HEADS, groups, HD)
    grad_value = jnp.einsum(
        "kgij,ikgd->jkd", prob_rows, grad_attended, preferred_element_type=jnp.float32
    )
    grad_probs = jnp.einsum(
        "ikgd,jkd->kgij", grad_attended, value_low, preferred_element_type=jnp.float32
    )
    inner_sum = jnp.sum(probs * grad_probs, axis=-1, keepdims=True)
    grad_scores = (probs * (grad_probs - inner_sum)).astype(jnp.bfloat16)
    grad_query = (
        jnp.einsum("kgij,jkd->ikgd", grad_scores, key_low, preferred_element_type=jnp.float32)
        * score_scale
    )
    grad_key = (
        jnp.einsum("kgij,ikgd->jkd", grad_scores, query_low, preferred_element_type=jnp.float32)
        * score_scale
    )
    grad_qkv = jnp.concatenate(
        [
            unrotate(grad_query.reshape(row_count, HEADS, HD), cosine, sine_table)
            .reshape(row_count, HEADS * HD)
            .astype(jnp.bfloat16),
            unrotate(grad_key, cosine, sine_table)
            .reshape(row_count, KV_HEADS * HD)
            .astype(jnp.bfloat16),
            grad_value.reshape(row_count, KV_HEADS * HD).astype(jnp.bfloat16),
        ],
        axis=1,
    )
    grad_wqkv = outer_sum(low_one_pair, token_pair(grad_qkv)).astype(jnp.bfloat16)
    grad_attention = jnp.concatenate([grad_wqkv, grad_wout], axis=1).reshape(
        chips, BLOCK, 2 * HEADS * HD + 2 * KV_HEADS * HD
    )

    grad_norm_one = gather_in(times_t(grad_qkv, w_qkv), count, width)
    grad_gain_one = jnp.sum(grad_norm_one * normed_one, axis=0)
    scaled_one = grad_norm_one * attention_gain
    grad_inputs = grad_middle + scale_one * (
        scaled_one - normed_one * jnp.mean(scaled_one * normed_one, axis=-1, keepdims=True)
    )
    gain_rows = jnp.concatenate(
        [grad_gain_one[None], grad_gain_two[None], jnp.zeros((6, D), jnp.float32)], axis=0
    )
    attention_sum, gate_up_sum, down_sum, gain_sums = scatter_chips(
        [grad_attention, grad_gate_up, grad_wdown.reshape(chips, units, D)], gain_rows
    )
    attention_sum = attention_sum[:width].astype(jnp.float32)

    gate_up_sum = gate_up_sum.reshape(2, BLOCK, 2 * chips * units)
    gate_up_got = other_core(take_core(gate_up_sum, 1 - core))
    gate_up_kept = take_core(gate_up_sum, core)
    halves = in_core_order(gate_up_kept[None], gate_up_got[None], 0)[:, :width]
    halves = halves.reshape(2, width, 2, chips, units).transpose(2, 1, 3, 0, 4).astype(jnp.float32)
    edge_key, edge_value = HEADS * HD, (HEADS + KV_HEADS) * HD
    return (
        layer_out,
        grad_inputs.astype(jnp.bfloat16),
        attention_sum[:, :edge_key].reshape(-1),
        attention_sum[:, edge_key:edge_value].reshape(-1),
        attention_sum[:, edge_value:wide_qkv].reshape(-1),
        attention_sum[:, wide_qkv:].reshape(-1),
        halves[0].reshape(-1),
        halves[1].reshape(-1),
        down_sum.astype(jnp.float32).reshape(-1),
        gain_sums[0],
        gain_sums[1],
    )


def solution(mesh):
    count = mesh.shape["fsdp"]
    whole_rows = count == 2 * CHIPS
    program = paired_on_device if whole_rows else on_device
    return jax.shard_map(
        program,
        mesh=mesh,
        in_specs=(
            P("fsdp", None),
            P("fsdp", None),
            P(),
            P(),
            P("fsdp"),
            P("fsdp"),
            P("fsdp"),
            P("fsdp"),
            P("fsdp"),
            P("fsdp"),
            P("fsdp"),
            P(),
            P(),
        ),
        out_specs=(
            P("fsdp", None),
            P("fsdp", None),
            P("fsdp"),
            P("fsdp"),
            P("fsdp"),
            P("fsdp"),
            P("fsdp"),
            P("fsdp"),
            P("fsdp"),
            P(),
            P(),
        ),
        check_vma=False,
    )
```
